256 devices in a mesh: arc: 16 (over x, y_lo, core), par: 16 (over y_hi, z).
Axes of the slice: x: 4, y: 4 (y_hi: 2, y_lo: 2; y = y_hi * 2 + y_lo), z: 8, core: 2. Of those that a mesh axis runs over, the one named last changes fastest.
Arguments:
- partials: bfloat16 [16, 3, 128, 8192], P('arc', None, 'par'), may hold values from -6 to 6
- epoch_index: int32 [16, 128], P('arc'), may hold values from 0 to 511, as said below
- whitening: float32 [16, 3, 128, 128], P('arc'), may hold values from -2 to 2, as said below
Outputs:
- normal_matrix: float32 [8192, 8192], P('arc', 'par')
The draws below stay inside these ranges and needn't reach their ends.
Inputs may be any that keep to these rules, and one draw needn't show every extreme that they name: `epoch_index`: in each arc the epoch indices rise strictly; the first is 0 and the last is 511. `whitening`: each block is lower triangular with diagonal entries between 1 and 2.
All inputs are finite; a program needn't handle non-finite values.
Results may differ from the reference program's by a relative error of at most 0.0003.
Values may be sent and summed in bfloat16 or wider, within the bound.
A program may use at most 128 MiB of HBM per device.

```python
import math
import jax
import jax.numpy as jnp
from jax import lax

P_SIZE = 8192
E = 128
ARCS = 16


def draw_epoch_index(key, part):
    epoch_span = 4 * E
    arc_keys = jax.random.split(jax.random.fold_in(key, 5), ARCS)

    def per_arc(arc_key):
        interior = jnp.sort(jax.random.permutation(arc_key, epoch_span - 2)[:E - 2]) + 1
        first_one = jnp.zeros((1,), jnp.int32)
        last_one = jnp.full((1,), epoch_span - 1, jnp.int32)
        return jnp.concatenate([first_one, interior.astype(jnp.int32), last_one])
    return jax.vmap(per_arc)(arc_keys)


def draw_whitening(key, part):
    first_key, second_key = jax.random.split(jax.random.fold_in(key, 11))
    diagonal = jax.random.uniform(first_key, (ARCS, 3, E), jnp.float32, 1.0, 2.0)
    lower_part = jax.random.normal(second_key, (ARCS, 3, E, E), jnp.float32) * (0.6 / math.sqrt(E))
    lower_part = jnp.tril(lower_part, -1)
    return lower_part + diagonal[..., None] * jnp.eye(E, dtype=jnp.float32)


def block_levels(key, dims, cuts, least, largest):
    gain = 1.0
    for position, shards_of in cuts:
        draws = jax.random.uniform(jax.random.fold_in(jax.random.fold_in(key, 6), position), (shards_of,), jnp.float32, least / len(cuts), largest / len(cuts))
        gain = gain * jnp.repeat(jnp.exp(draws), dims[position] // shards_of).reshape((-1,) + (1,) * (len(dims) - 1 - position))
    return gain


def scatter_about(own_key, extent, spread, bound, shards=(), kind=jnp.bfloat16):
    result = jax.random.normal(own_key, extent, jnp.float32) * spread
    if len(shards) > 0:
        result = block_levels(own_key, extent, shards, -0.22, 0.18) * result
    return jnp.clip(result, min=-bound, max=bound).astype(kind)


def setup_inputs(seed: int = 0) -> dict:
    keys = jax.random.split(jax.random.key(seed), 4)
    partials = scatter_about(keys[0], (ARCS, 3, E, P_SIZE), 1.0, 6.0, ((0, 16), (2, 16)))
    epoch_index = draw_epoch_index(jax.random.fold_in(keys[3], 71), 0)
    whitening = draw_whitening(jax.random.fold_in(keys[3], 71), 0)
    return dict(partials=partials, epoch_index=epoch_index, whitening=whitening)


KERNEL_GAIN = 8.0

def mixing_matrices(epoch_index, whitening, epochs, row_scale):
    times_arc = epoch_index.astype(jnp.float32) / jnp.float32(4 * epochs - 1)
    later_time = times_arc[:, :, None]
    earlier_time = times_arc[:, None, :]
    green_part = jnp.minimum(later_time, earlier_time) * (1.0 - jnp.maximum(later_time, earlier_time))
    kernel = jnp.eye(epochs, dtype=jnp.float32)[None] + KERNEL_GAIN / epochs * green_part
    mixing = jnp.einsum('acij,ajk->acik', whitening, kernel, precision=lax.Precision.HIGHEST)
    return mixing * row_scale

def reference(partials, epoch_index, whitening):
    row_scale = 1.0 / math.sqrt(3 * E * ARCS)
    mixing = mixing_matrices(epoch_index, whitening, E, row_scale)
    panels = jnp.einsum('acij,acjk->acik', mixing, partials.astype(jnp.float32), precision=lax.Precision.HIGHEST)
    stacked = panels.reshape(-1, P_SIZE)
    return lax.dot_general(stacked, stacked, (((0,), (0,)), ((), ())), precision=lax.Precision.HIGHEST, preferred_element_type=jnp.float32)
```

```python
import math

import jax
import jax.numpy as jnp
from jax import lax
from jax.experimental import pallas as pl
from jax.experimental.pallas import tpu as pltpu
from jax.sharding import PartitionSpec as P

KERNEL_GAIN = 8.0
MESH = pl.DeviceIdType.MESH
EARLY = 8
N_SEM = 80


def kernel(part_ref, epoch_ref, white_ref, out_ref, blocks, rows, cols, mixers, q_all, send_sem, recv_sem, bulk_send, bulk_recv):
    a = lax.axis_index("arc")
    p = lax.axis_index("par")
    x, yl, core = a // 4, (a // 2) % 2, a % 2
    yh, z = p // 8, p % 8
    other_core = (x * 4 + yl * 2 + 1 - core, p)
    yl_partner = (x * 4 + (1 - yl) * 2 + core, p)
    yh_partner = (a, (1 - yh) * 8 + z)

    def arc_at(dx, same_yl, same_core):
        return (
            ((x + dx + 4) % 4) * 4
            + (yl if same_yl else 1 - yl) * 2
            + (core if same_core else 1 - core)
        )

    def par_at(same_yh, dz):
        return (yh if same_yh else 1 - yh) * 8 + (z + dz + 8) % 8

    barrier = pltpu.get_barrier_semaphore()

    def greet(k, _):
        pl.semaphore_signal(barrier, inc=1, device_id=((a + k) % 16, p), device_id_type=MESH)
        pl.semaphore_signal(barrier, inc=1, device_id=(a, (p + k) % 16), device_id_type=MESH)
        return 0

    lax.fori_loop(1, 16, greet, 0)

    for c in range(3):
        for b in range(16):
            piece = part_ref[0, c, :, b * 512 : (b + 1) * 512].astype(jnp.float32)
            unit = jnp.concatenate([piece[:, :256], piece[:, 256:]], axis=0)
            blocks[b, c * 16 : (c + 1) * 16, :] = unit.astype(jnp.bfloat16)

    pl.semaphore_wait(barrier, 30)

    def send_rows(k, _):
        b = (a + k) % 16
        pltpu.make_async_remote_copy(
            src_ref=blocks.at[b], dst_ref=rows.at[p, a], send_sem=bulk_send.at[0], recv_sem=bulk_recv.at[0],
            device_id=(b, p), device_id_type=MESH,
        ).start()
        return 0

    def send_cols(k, _):
        b = (p + k) % 16
        pltpu.make_async_remote_copy(
            src_ref=blocks.at[b], dst_ref=cols.at[a, p], send_sem=bulk_send.at[1], recv_sem=bulk_recv.at[1],
            device_id=(a, b), device_id_type=MESH,
        ).start()
        return 0

    lax.fori_loop(1, 16, send_rows, 0)
    lax.fori_loop(1, 16, send_cols, 0)
    rows[p, a] = blocks[a]
    cols[a, p] = blocks[p]

    row_scale = 1.0 / math.sqrt(6144)
    times = epoch_ref[...].astype(jnp.float32) / jnp.float32(511)
    later = jnp.broadcast_to(times, (128, 128))
    earlier = jnp.transpose(later)
    i = lax.broadcasted_iota(jnp.int32, (128, 128), 0)
    j = lax.broadcasted_iota(jnp.int32, (128, 128), 1)
    eye = jnp.where(i == j, 1.0, 0.0).astype(jnp.float32)
    green = jnp.minimum(later, earlier) * (1.0 - jnp.maximum(later, earlier))
    integral = eye + KERNEL_GAIN / 128 * green
    for c in range(3):
        m = jnp.dot(white_ref[0, c], integral, precision=lax.Precision.HIGHEST, preferred_element_type=jnp.float32) * row_scale
        g = jnp.dot(jnp.transpose(m), m, precision=lax.Precision.HIGHEST, preferred_element_type=jnp.float32)
        high = g.astype(jnp.bfloat16)
        low = (g - high.astype(jnp.float32)).astype(jnp.bfloat16)
        mixers[a, c * 128 : (c + 1) * 128, :] = jnp.concatenate([high, low], axis=1)

    counter = [0]
    started = []

    class Link:
        def __init__(self, target, src, landing):
            self.n = counter[0]
            counter[0] += 1
            self.target, self.src, self.landing = target, src, landing

        def start(self):
            self.copy = pltpu.make_async_remote_copy(
                src_ref=self.src, dst_ref=self.src, send_sem=send_sem.at[self.n], recv_sem=recv_sem.at[self.n],
                device_id=self.target, device_id_type=MESH,
            )
            self.copy.start()
            started.append(self.copy)

        def arrived(self):
            pltpu.make_async_remote_copy(
                src_ref=self.landing, dst_ref=self.landing, send_sem=send_sem.at[self.n], recv_sem=recv_sem.at[self.n],
                device_id=self.target, device_id_type=MESH,
            ).wait_recv()

    tasks = []

    def at(time, act):
        tasks.append((time, len(tasks), act))

    def row_part(part, dz, half=None):
        same = part != "E1"
        lo, n = (0, EARLY) if part in ("E0", "E1") else (EARLY, 16 - EARLY)
        if half is not None:
            n1 = n // 2
            lo, n = (lo, n1) if half == 0 else (lo + n1, n - n1)
        return rows.at[par_at(same, dz), pl.ds(lo, n)]

    parts = ("L", "E0", "E1")
    z_to = {1: (a, par_at(True, 1)), -1: (a, par_at(True, -1))}
    ring = {}
    for step in range(1, 5):
        for part in parts:
            for d in (1, -1):
                half = None if step < 4 else (0 if d == 1 else 1)
                ring[step, part, d] = Link(
                    z_to[d], row_part(part, -d * (step - 1), half), row_part(part, -d * step, half)
                )
    cross_early = Link(yh_partner, rows.at[p, pl.ds(0, EARLY)], rows.at[par_at(False, 0), pl.ds(0, EARLY)])
    late = pl.ds(EARLY, 16 - EARLY)
    cross_late = {
        dz: Link(yh_partner, rows.at[par_at(True, dz), late], rows.at[par_at(False, dz), late])
        for dz in (0, 1, -1, 2, -2, 3, -3, 4)
    }

    def rows_ready():
        pltpu.make_async_copy(rows.at[p, pl.ds(0, 15)], rows.at[p, pl.ds(0, 15)], bulk_recv.at[0]).wait()
        cross_early.start()
        for part in ("L", "E0"):
            for d in (1, -1):
                ring[1, part, d].start()
        cross_late[0].start()

    at(5, rows_ready)

    def early_crossed():
        cross_early.arrived()
        for d in (1, -1):
            ring[1, "E1", d].start()

    at(9.6, early_crossed)

    def ring_arrival(step, part, d):
        ring[step, part, d].arrived()
        if step < 4:
            ring[step + 1, part, d].start()
        if part == "L" and step < 4:
            cross_late[-d * step].start()

    for step in range(1, 5):
        for n, part in enumerate(parts):
            for d in (1, -1):
                time = 5 + 4.2 * (1 + 3 * (step - 1) + n) if step < 4 else 43 + 2.1 * (n + 1)
                at(time, lambda s=step, q=part, d=d: ring_arrival(s, q, d))

    def last_late():
        cross_late[4].start()

    at(45.2, last_late)

    def gather_over_arc(buf, extent, time, first):
        def piece(arc, half=None):
            if half is None:
                return buf.at[arc]
            n = extent // 2
            return buf.at[arc, pl.ds(half * n, n)]

        x_to = {1: (arc_at(1, True, True), p), -1: (arc_at(-1, True, True), p)}
        to_yl = Link(yl_partner, piece(a), piece(arc_at(0, False, True)))
        hops, cores = {}, {}
        for mine in (True, False):
            for d in (1, -1):
                hops[1, mine, d] = Link(x_to[d], piece(arc_at(0, mine, True)), piece(arc_at(-d, mine, True)))
                half = 0 if d == 1 else 1
                hops[2, mine, d] = Link(x_to[d], piece(arc_at(-d, mine, True), half), piece(arc_at(2, mine, True), half))
            cores[0, mine] = Link(other_core, piece(arc_at(0, mine, True)), piece(arc_at(0, mine, False)))
            for d in (1, -1):
                cores[1, mine, d] = Link(other_core, piece(arc_at(-d, mine, True)), piece(arc_at(-d, mine, False)))
                half = 0 if d == 1 else 1
                cores[2, mine, d] = Link(other_core, piece(arc_at(2, mine, True), half), piece(arc_at(2, mine, False), half))

        def begin():
            first()
            to_yl.start()
            for d in (1, -1):
                hops[1, True, d].start()
            cores[0, True].start()

        def yl_arrival():
            to_yl.arrived()
            for d in (1, -1):
                hops[1, False, d].start()
            cores[0, False].start()

        def hop_arrival(dist, mine, d):
            hops[dist, mine, d].arrived()
            if dist == 1:
                hops[2, mine, d].start()
            cores[dist, mine, d].start()

        at(time["begin"], begin)
        at(time["yl"], yl_arrival)
        for mine in (True, False):
            for dist in (1, 2):
                for d in (1, -1):
                    at(time[dist, mine], lambda s=dist, m=mine, d=d: hop_arrival(s, m, d))

        def wait_group(dist, mine):
            if dist == 0:
                cores[0, mine].arrived()
            else:
                for d in (1, -1):
                    cores[dist, mine, d].arrived()

        return wait_group

    wait_g = gather_over_arc(
        mixers, 384,
        {"begin": 4, "yl": 8, (1, True): 8.5, (1, False): 13, (2, True): 15, (2, False): 17.5},
        lambda: None,
    )

    def cols_ready():
        pltpu.make_async_copy(cols.at[a, pl.ds(0, 15)], cols.at[a, pl.ds(0, 15)], bulk_recv.at[1]).wait()

    wait_c = gather_over_arc(
        cols, 16,
        {"begin": 10, "yl": 19, (1, True): 24.5, (1, False): 33, (2, True): 37.1, (2, False): 41.3},
        cols_ready,
    )

    def mix(arc):
        for c in range(3):
            unit = cols[arc, :, c * 16 : (c + 1) * 16, :].astype(jnp.float32).reshape(16, 2, 8, 256)
            b = jnp.concatenate([unit[:, 0].reshape(128, 256), unit[:, 1].reshape(128, 256)], axis=1).astype(jnp.bfloat16)
            q = jnp.dot(
                mixers[arc, c * 128 : (c + 1) * 128, :], jnp.concatenate([b, b], axis=0), preferred_element_type=jnp.float32
            )
            q_all[:, arc * 3 + c] = q.reshape(16, 8, 512)

    def mix_group(dist, mine):
        waits = []
        if dist < 2:
            wait_g(dist, mine), wait_c(dist, mine)
        else:
            wait_g(dist, mine), wait_c(dist, mine)
        yl_of = yl if mine else 1 - yl
        if dist == 1:
            def body(k, _):
                dx = (k // 2) * 2 - 1
                mix(((x + dx + 4) % 4) * 4 + yl_of * 2 + k % 2)
                return 0
            lax.fori_loop(0, 4, body, 0)
        else:
            def body(k, _):
                mix(((x + dist) % 4) * 4 + yl_of * 2 + k)
                return 0
            lax.fori_loop(0, 2, body, 0)

    at(20, lambda: mix_group(0, True))
    at(22, lambda: mix_group(0, False))
    at(28, lambda: mix_group(1, True))
    at(35, lambda: mix_group(1, False))
    at(38.5, lambda: mix_group(2, True))
    at(42.5, lambda: mix_group(2, False))

    def accumulate(par, first=False):
        unit = rows[par].astype(jnp.float32).reshape(16, 3, 2, 8, 256)
        b = jnp.concatenate([unit[:, :, 0].reshape(384, 256), unit[:, :, 1].reshape(384, 256)], axis=1).astype(jnp.bfloat16)
        bt = jnp.transpose(b)
        q = q_all[par].reshape(384, 512)
        high = q.astype(jnp.bfloat16)
        low = (q - high.astype(jnp.float32)).astype(jnp.bfloat16)
        term = jnp.dot(
            jnp.concatenate([bt, bt], axis=1), jnp.concatenate([high, low], axis=0), preferred_element_type=jnp.float32
        )
        out_ref[...] += term

    def accumulate_group(dist):
        if dist == 0:
            cross_late[0].arrived()
            out_ref[...] = jnp.zeros_like(out_ref)
        elif dist < 4:
            cross_late[dist].arrived()
            cross_late[-dist].arrived()
        else:
            cross_late[4].arrived()
        if dist in (0, 4):
            def body(k, _):
                accumulate(k * 8 + (z + dist) % 8)
                return 0
            lax.fori_loop(0, 2, body, 0)
        else:
            def body(k, _):
                dz = dist * ((k // 2) * 2 - 1)
                accumulate((k % 2) * 8 + (z + dz + 8) % 8)
                return 0
            lax.fori_loop(0, 4, body, 0)

    at(42.6, lambda: accumulate_group(0))
    at(43.5, lambda: accumulate_group(1))
    at(46, lambda: accumulate_group(2))
    at(49.4, lambda: accumulate_group(3))
    at(52, lambda: accumulate_group(4))

    for _, _, act in sorted(tasks, key=lambda t: t[:2]):
        act()

    assert counter[0] <= N_SEM
    for n in (0, 1):
        pltpu.make_async_copy(blocks.at[pl.ds(0, 15)], blocks.at[pl.ds(0, 15)], bulk_send.at[n]).wait()
    for copy in started:
        copy.wait_send()


def on_device(partials, epoch_index, whitening):
    vmem = pl.BlockSpec(memory_space=pltpu.VMEM)
    return pl.pallas_call(
        kernel,
        out_shape=jax.ShapeDtypeStruct((512, 512), jnp.float32),
        in_specs=[vmem, vmem, vmem],
        out_specs=vmem,
        scratch_shapes=[
            pltpu.VMEM((16, 48, 256), jnp.bfloat16),
            pltpu.VMEM((16, 16, 48, 256), jnp.bfloat16),
            pltpu.VMEM((16, 16, 48, 256), jnp.bfloat16),
            pltpu.VMEM((16, 384, 256), jnp.bfloat16),
            pltpu.VMEM((16, 48, 8, 512), jnp.float32),
            pltpu.SemaphoreType.DMA((N_SEM,)),
            pltpu.SemaphoreType.DMA((N_SEM,)),
            pltpu.SemaphoreType.DMA((2,)),
            pltpu.SemaphoreType.DMA((2,)),
        ],
        compiler_params=pltpu.CompilerParams(
            collective_id=0, has_side_effects=True, vmem_limit_bytes=56 * 2**20
        ),
    )(partials, epoch_index, whitening)


def solution(mesh):
    placed = (P("arc", None, "par", None), P("arc", None), P("arc", None, None, None))
    return jax.shard_map(
        on_device, mesh=mesh, in_specs=placed, out_specs=P("arc", "par"), check_vma=False
    )
```

```python
import math

import jax
import jax.numpy as jnp
from jax import lax
from jax.experimental import pallas as pl
from jax.experimental.pallas import tpu as pltpu
from jax.sharding import PartitionSpec as P

KERNEL_GAIN = 8.0
MESH = pl.DeviceIdType.MESH
EARLY = 8
N_SEM = 80
ORDER = (
    ("G", "begin"), ("C", "begin"), ("G", 1, True, 1), ("G", 1, True, -1), "rows", ("G", 2, True, 1),
    ("G", "yl"), ("mix", 0, True), ("G", 2, True, -1), ("z", 1, "E0", -1), ("z", 1, "E0", 1),
    ("z", 1, "L", -1), ("z", 1, "L", 1), ("G", 1, False, 1), "early", ("G", 1, False, -1), ("C", 1, True, 1),
    ("C", 1, True, -1), ("G", 2, False, -1), ("G", 2, False, 1), ("mix", 1, True), ("z", 2, "L", 1),
    ("z", 2, "L", -1), ("z", 2, "E0", 1), ("C", 2, True, -1), ("z", 1, "E1", 1), ("z", 2, "E0", -1),
    ("C", 2, True, 1), ("z", 1, "E1", -1), ("mix", 2, True), ("C", "yl"), ("z", 3, "L", 1), ("z", 3, "L", -1),
    ("mix", 0, False), ("z", 3, "E0", 1), ("z", 2, "E1", 1), ("z", 2, "E1", -1), ("z", 3, "E0", -1),
    ("C", 1, False, 1), ("C", 1, False, -1), ("mix", 1, False), ("z", 4, "L", -1), ("z", 4, "L", 1), "last",
    ("C", 2, False, 1), ("C", 2, False, -1), ("mix", 2, False), ("acc", 0), ("z", 3, "E1", -1),
    ("z", 3, "E1", 1), ("acc", 1), ("acc", 3), ("z", 4, "E0", -1), ("z", 4, "E1", -1), ("z", 4, "E0", 1),
    ("z", 4, "E1", 1), ("acc", 4), ("acc", 2),
)


def kernel(part_ref, epoch_ref, white_ref, out_ref, blocks, rows, cols, mixers, q_all, send_sem, recv_sem, bulk_send, bulk_recv):
    a = lax.axis_index("arc")
    p = lax.axis_index("par")
    x, yl, core = a // 4, (a // 2) % 2, a % 2
    yh, z = p // 8, p % 8
    other_core = (x * 4 + yl * 2 + 1 - core, p)
    yl_partner = (x * 4 + (1 - yl) * 2 + core, p)
    yh_partner = (a, (1 - yh) * 8 + z)

    def arc_at(dx, same_yl, same_core):
        return (
            ((x + dx + 4) % 4) * 4
            + (yl if same_yl else 1 - yl) * 2
            + (core if same_core else 1 - core)
        )

    def par_at(same_yh, dz):
        return (yh if same_yh else 1 - yh) * 8 + (z + dz + 8) % 8

    barrier = pltpu.get_barrier_semaphore()

    def greet(k, _):
        pl.semaphore_signal(barrier, inc=1, device_id=((a + k) % 16, p), device_id_type=MESH)
        pl.semaphore_signal(barrier, inc=1, device_id=(a, (p + k) % 16), device_id_type=MESH)
        return 0

    lax.fori_loop(1, 16, greet, 0)

    for c in range(3):
        for b in range(16):
            piece = part_ref[0, c, :, b * 512 : (b + 1) * 512].astype(jnp.float32)
            unit = jnp.concatenate([piece[:, :256], piece[:, 256:]], axis=0)
            blocks[b, c * 16 : (c + 1) * 16, :] = unit.astype(jnp.bfloat16)

    pl.semaphore_wait(barrier, 30)

    def send_rows(k, _):
        b = (a + k) % 16
        pltpu.make_async_remote_copy(
            src_ref=blocks.at[b], dst_ref=rows.at[p, a], send_sem=bulk_send.at[0], recv_sem=bulk_recv.at[0],
            device_id=(b, p), device_id_type=MESH,
        ).start()
        return 0

    def send_cols(k, _):
        b = (p + k) % 16
        pltpu.make_async_remote_copy(
            src_ref=blocks.at[b], dst_ref=cols.at[a, p], send_sem=bulk_send.at[1], recv_sem=bulk_recv.at[1],
            device_id=(a, b), device_id_type=MESH,
        ).start()
        return 0

    lax.fori_loop(1, 16, send_rows, 0)
    lax.fori_loop(1, 16, send_cols, 0)
    rows[p, a] = blocks[a]
    cols[a, p] = blocks[p]

    row_scale = 1.0 / math.sqrt(6144)
    times = epoch_ref[...].astype(jnp.float32) / jnp.float32(511)
    later = jnp.broadcast_to(times, (128, 128))
    earlier = jnp.transpose(later)
    i = lax.broadcasted_iota(jnp.int32, (128, 128), 0)
    j = lax.broadcasted_iota(jnp.int32, (128, 128), 1)
    eye = jnp.where(i == j, 1.0, 0.0).astype(jnp.float32)
    green = jnp.minimum(later, earlier) * (1.0 - jnp.maximum(later, earlier))
    integral = eye + KERNEL_GAIN / 128 * green
    for c in range(3):
        m = jnp.dot(white_ref[0, c], integral, precision=lax.Precision.HIGHEST, preferred_element_type=jnp.float32) * row_scale
        g = jnp.dot(jnp.transpose(m), m, precision=lax.Precision.HIGHEST, preferred_element_type=jnp.float32)
        high = g.astype(jnp.bfloat16)
        low = (g - high.astype(jnp.float32)).astype(jnp.bfloat16)
        mixers[a, c * 128 : (c + 1) * 128, :] = jnp.concatenate([high, low], axis=1)

    counter = [0]
    started = []

    class Link:
        def __init__(self, target, src, landing):
            self.n = counter[0]
            counter[0] += 1
            self.target, self.src, self.landing = target, src, landing

        def start(self):
            self.copy = pltpu.make_async_remote_copy(
                src_ref=self.src, dst_ref=self.src, send_sem=send_sem.at[self.n], recv_sem=recv_sem.at[self.n],
                device_id=self.target, device_id_type=MESH,
            )
            self.copy.start()
            started.append(self.copy)

        def arrived(self):
            pltpu.make_async_remote_copy(
                src_ref=self.landing, dst_ref=self.landing, send_sem=send_sem.at[self.n], recv_sem=recv_sem.at[self.n],
                device_id=self.target, device_id_type=MESH,
            ).wait_recv()

    tasks = {}

    def at(key, act):
        tasks[key] = act

    def row_part(part, dz, half=None):
        same = part != "E1"
        lo, n = (0, EARLY) if part in ("E0", "E1") else (EARLY, 16 - EARLY)
        if half is not None:
            n1 = n // 2
            lo, n = (lo, n1) if half == 0 else (lo + n1, n - n1)
        return rows.at[par_at(same, dz), pl.ds(lo, n)]

    parts = ("L", "E0", "E1")
    z_to = {1: (a, par_at(True, 1)), -1: (a, par_at(True, -1))}
    ring = {}
    for step in range(1, 5):
        for part in parts:
            for d in (1, -1):
                half = None if step < 4 else (0 if d == 1 else 1)
                ring[step, part, d] = Link(
                    z_to[d], row_part(part, -d * (step - 1), half), row_part(part, -d * step, half)
                )
    cross_early = Link(yh_partner, rows.at[p, pl.ds(0, EARLY)], rows.at[par_at(False, 0), pl.ds(0, EARLY)])
    late = pl.ds(EARLY, 16 - EARLY)
    cross_late = {
        dz: Link(yh_partner, rows.at[par_at(True, dz), late], rows.at[par_at(False, dz), late])
        for dz in (0, 1, -1, 2, -2, 3, -3, 4)
    }

    def rows_ready():
        pltpu.make_async_copy(rows.at[p, pl.ds(0, 15)], rows.at[p, pl.ds(0, 15)], bulk_recv.at[0]).wait()
        cross_early.start()
        for part in ("L", "E0"):
            for d in (1, -1):
                ring[1, part, d].start()
        cross_late[0].start()

    at("rows", rows_ready)

    def early_crossed():
        cross_early.arrived()
        for d in (1, -1):
            ring[1, "E1", d].start()

    at("early", early_crossed)

    def ring_arrival(step, part, d):
        ring[step, part, d].arrived()
        if step < 4:
            ring[step + 1, part, d].start()
        if part == "L" and step < 4:
            cross_late[-d * step].start()

    for step in range(1, 5):
        for part in parts:
            for d in (1, -1):
                at(("z", step, part, d), lambda s=step, q=part, d=d: ring_arrival(s, q, d))

    def last_late():
        cross_late[4].start()

    at("last", last_late)

    def gather_over_arc(name, buf, extent, first):
        def piece(arc, half=None):
            if half is None:
                return buf.at[arc]
            n = extent // 2
            return buf.at[arc, pl.ds(half * n, n)]

        x_to = {1: (arc_at(1, True, True), p), -1: (arc_at(-1, True, True), p)}
        to_yl = Link(yl_partner, piece(a), piece(arc_at(0, False, True)))
        hops, cores = {}, {}
        for mine in (True, False):
            for d in (1, -1):
                hops[1, mine, d] = Link(x_to[d], piece(arc_at(0, mine, True)), piece(arc_at(-d, mine, True)))
                half = 0 if d == 1 else 1
                hops[2, mine, d] = Link(x_to[d], piece(arc_at(-d, mine, True), half), piece(arc_at(2, mine, True), half))
            cores[0, mine] = Link(other_core, piece(arc_at(0, mine, True)), piece(arc_at(0, mine, False)))
            for d in (1, -1):
                cores[1, mine, d] = Link(other_core, piece(arc_at(-d, mine, True)), piece(arc_at(-d, mine, False)))
                half = 0 if d == 1 else 1
                cores[2, mine, d] = Link(other_core, piece(arc_at(2, mine, True), half), piece(arc_at(2, mine, False), half))

        def begin():
            first()
            to_yl.start()
            for d in (1, -1):
                hops[1, True, d].start()
            cores[0, True].start()

        def yl_arrival():
            to_yl.arrived()
            for d in (1, -1):
                hops[1, False, d].start()
            cores[0, False].start()

        def hop_arrival(dist, mine, d):
            hops[dist, mine, d].arrived()
            if dist == 1:
                hops[2, mine, d].start()
            cores[dist, mine, d].start()

        at((name, "begin"), begin)
        at((name, "yl"), yl_arrival)
        for mine in (True, False):
            for dist in (1, 2):
                for d in (1, -1):
                    at((name, dist, mine, d), lambda s=dist, m=mine, d=d: hop_arrival(s, m, d))

        def wait_group(dist, mine):
            if dist == 0:
                cores[0, mine].arrived()
            else:
                for d in (1, -1):
                    cores[dist, mine, d].arrived()

        return wait_group

    wait_g = gather_over_arc("G", mixers, 384, lambda: None)

    def cols_ready():
        pltpu.make_async_copy(cols.at[a, pl.ds(0, 15)], cols.at[a, pl.ds(0, 15)], bulk_recv.at[1]).wait()

    wait_c = gather_over_arc("C", cols, 16, cols_ready)

    def mix(arc):
        for c in range(3):
            unit = cols[arc, :, c * 16 : (c + 1) * 16, :].astype(jnp.float32).reshape(16, 2, 8, 256)
            b = jnp.concatenate([unit[:, 0].reshape(128, 256), unit[:, 1].reshape(128, 256)], axis=1).astype(jnp.bfloat16)
            q = jnp.dot(
                mixers[arc, c * 128 : (c + 1) * 128, :], jnp.concatenate([b, b], axis=0), preferred_element_type=jnp.float32
            )
            q_all[:, arc * 3 + c] = q.reshape(16, 8, 512)

    def mix_group(dist, mine):
        wait_g(dist, mine)
        wait_c(dist, mine)
        yl_of = yl if mine else 1 - yl
        if dist == 1:
            def body(k, _):
                dx = (k // 2) * 2 - 1
                mix(((x + dx + 4) % 4) * 4 + yl_of * 2 + k % 2)
                return 0
            lax.fori_loop(0, 4, body, 0)
        else:
            def body(k, _):
                mix(((x + dist) % 4) * 4 + yl_of * 2 + k)
                return 0
            lax.fori_loop(0, 2, body, 0)

    for dist in range(3):
        for mine in (True, False):
            at(("mix", dist, mine), lambda s=dist, m=mine: mix_group(s, m))

    def accumulate(par):
        unit = rows[par].astype(jnp.float32).reshape(16, 3, 2, 8, 256)
        b = jnp.concatenate([unit[:, :, 0].reshape(384, 256), unit[:, :, 1].reshape(384, 256)], axis=1).astype(jnp.bfloat16)
        bt = jnp.transpose(b)
        q = q_all[par].reshape(384, 512)
        high = q.astype(jnp.bfloat16)
        low = (q - high.astype(jnp.float32)).astype(jnp.bfloat16)
        term = jnp.dot(
            jnp.concatenate([bt, bt], axis=1), jnp.concatenate([high, low], axis=0), preferred_element_type=jnp.float32
        )
        out_ref[...] += term

    def accumulate_group(dist):
        if dist == 0:
            cross_late[0].arrived()
            out_ref[...] = jnp.zeros_like(out_ref)
        elif dist < 4:
            cross_late[dist].arrived()
            cross_late[-dist].arrived()
        else:
            cross_late[4].arrived()
        if dist in (0, 4):
            def body(k, _):
                accumulate(k * 8 + (z + dist) % 8)
                return 0
            lax.fori_loop(0, 2, body, 0)
        else:
            def body(k, _):
                dz = dist * ((k // 2) * 2 - 1)
                accumulate((k % 2) * 8 + (z + dz + 8) % 8)
                return 0
            lax.fori_loop(0, 4, body, 0)

    for dist in range(5):
        at(("acc", dist), lambda s=dist: accumulate_group(s))

    assert sorted(map(str, tasks)) == sorted(map(str, ORDER))
    for key in ORDER:
        tasks[key]()

    assert counter[0] <= N_SEM
    for n in (0, 1):
        pltpu.make_async_copy(blocks.at[pl.ds(0, 15)], blocks.at[pl.ds(0, 15)], bulk_send.at[n]).wait()
    for copy in started:
        copy.wait_send()


def on_device(partials, epoch_index, whitening):
    vmem = pl.BlockSpec(memory_space=pltpu.VMEM)
    return pl.pallas_call(
        kernel,
        out_shape=jax.ShapeDtypeStruct((512, 512), jnp.float32),
        in_specs=[vmem, vmem, vmem],
        out_specs=vmem,
        scratch_shapes=[
            pltpu.VMEM((16, 48, 256), jnp.bfloat16),
            pltpu.VMEM((16, 16, 48, 256), jnp.bfloat16),
            pltpu.VMEM((16, 16, 48, 256), jnp.bfloat16),
            pltpu.VMEM((16, 384, 256), jnp.bfloat16),
            pltpu.VMEM((16, 48, 8, 512), jnp.float32),
            pltpu.SemaphoreType.DMA((N_SEM,)),
            pltpu.SemaphoreType.DMA((N_SEM,)),
            pltpu.SemaphoreType.DMA((2,)),
            pltpu.SemaphoreType.DMA((2,)),
        ],
        compiler_params=pltpu.CompilerParams(
            collective_id=0, has_side_effects=True, vmem_limit_bytes=56 * 2**20
        ),
    )(partials, epoch_index, whitening)


def solution(mesh):
    placed = (P("arc", None, "par", None), P("arc", None), P("arc", None, None, None))
    return jax.shard_map(
        on_device, mesh=mesh, in_specs=placed, out_specs=P("arc", "par"), check_vma=False
    )
```

```python
import math

import jax
import jax.numpy as jnp
from jax import lax
from jax.experimental import pallas as pl
from jax.experimental.pallas import tpu as pltpu
from jax.sharding import PartitionSpec as P

KERNEL_GAIN = 8.0
MESH = pl.DeviceIdType.MESH
EARLY = 8
N_SEM = 80
GROUPS = ((-2, 1, 5), (-3, 6, 2), (4, 1, 1))
ORDER = (
    "clear", ("G", "begin"), ("G", 1, True, 1), ("G", 1, True, -1), "rows", ("C", "begin"), ("mix", 0, True),
    ("G", 2, True, 1), ("G", 2, True, -1), ("G", "yl"), "early", ("z", 1, "E0", 1), ("z", 1, "L", 1),
    ("late", 0), ("z", 1, "L", -1), ("late", 1), ("G", 1, False, 1), ("G", 1, False, -1), ("C", 1, True, -1),
    ("z", 1, "E0", -1), ("late", -1), ("C", 1, True, 1), ("mix", 1, True), ("G", 2, False, -1),
    ("C", 2, True, -1), ("z", 1, "E1", -1), ("C", "yl"), ("C", 2, True, 1), ("z", 1, "E1", 1),
    ("z", 2, "L", 1), ("late", -2), ("z", 2, "L", -1), ("late", 2), ("z", 2, "E0", 1), ("mix", 2, True),
    ("turn", 0), ("turn", 1), ("G", 2, False, 1), ("mix", 0, False), ("z", 2, "E0", -1), ("C", 1, False, 1),
    ("C", 1, False, -1), ("turn", -1), ("z", 2, "E1", 1), ("z", 2, "E1", -1), ("mix", 1, False),
    ("z", 3, "L", -1), ("late", 3), ("z", 3, "L", 1), ("turn", 2), ("turn", -2), ("z", 3, "E0", -1),
    ("late", -3), ("C", 2, False, 1), ("z", 3, "E0", 1), ("C", 2, False, -1), ("mix", 2, False),
    ("sum", (-2, 1, 5)), ("z", 4, "L", -1), ("z", 3, "E1", -1), ("z", 4, "E0", -1), ("z", 4, "L", 1),
    ("late", 4), ("z", 3, "E1", 1), ("turn", 3), ("z", 4, "E0", 1), ("z", 4, "E1", -1), ("turn", -3),
    ("sum", (-3, 6, 2)), ("z", 4, "E1", 1), ("turn", 4), ("sum", (4, 1, 1)),
)


def kernel(part_ref, epoch_ref, white_ref, out_ref, blocks, rows, cols, mixers, rows_t, q_high, q_low, send_sem, recv_sem, bulk_send, bulk_recv):
    a = lax.axis_index("arc")
    p = lax.axis_index("par")
    x, yl, core = a // 4, (a // 2) % 2, a % 2
    yh, z = p // 8, p % 8
    other_core = (x * 4 + yl * 2 + 1 - core, p)
    yl_partner = (x * 4 + (1 - yl) * 2 + core, p)
    yh_partner = (a, (1 - yh) * 8 + z)

    def arc_at(dx, same_yl, same_core):
        return (
            ((x + dx + 4) % 4) * 4
            + (yl if same_yl else 1 - yl) * 2
            + (core if same_core else 1 - core)
        )

    def par_at(same_yh, dz):
        return (yh if same_yh else 1 - yh) * 8 + (z + dz + 8) % 8

    barrier = pltpu.get_barrier_semaphore()

    def greet(k, _):
        pl.semaphore_signal(barrier, inc=1, device_id=((a + k) % 16, p), device_id_type=MESH)
        pl.semaphore_signal(barrier, inc=1, device_id=(a, (p + k) % 16), device_id_type=MESH)
        return 0

    lax.fori_loop(1, 16, greet, 0)

    for c in range(3):
        for b in range(16):
            piece = part_ref[0, c, :, b * 512 : (b + 1) * 512].astype(jnp.float32)
            unit = jnp.concatenate([piece[:, :256], piece[:, 256:]], axis=0)
            blocks[b, c * 16 : (c + 1) * 16, :] = unit.astype(jnp.bfloat16)

    pl.semaphore_wait(barrier, 30)

    def send_rows(k, _):
        b = (a + k) % 16
        pltpu.make_async_remote_copy(
            src_ref=blocks.at[b], dst_ref=rows.at[p, a], send_sem=bulk_send.at[0], recv_sem=bulk_recv.at[0],
            device_id=(b, p), device_id_type=MESH,
        ).start()
        return 0

    def send_cols(k, _):
        b = (p + k) % 16
        pltpu.make_async_remote_copy(
            src_ref=blocks.at[b], dst_ref=cols.at[a, p], send_sem=bulk_send.at[1], recv_sem=bulk_recv.at[1],
            device_id=(a, b), device_id_type=MESH,
        ).start()
        return 0

    lax.fori_loop(1, 16, send_rows, 0)
    lax.fori_loop(1, 16, send_cols, 0)
    rows[p, a] = blocks[a]
    cols[a, p] = blocks[p]

    row_scale = 1.0 / math.sqrt(6144)
    times = epoch_ref[...].astype(jnp.float32) / jnp.float32(511)
    later = jnp.broadcast_to(times, (128, 128))
    earlier = jnp.transpose(later)
    i = lax.broadcasted_iota(jnp.int32, (128, 128), 0)
    j = lax.broadcasted_iota(jnp.int32, (128, 128), 1)
    eye = jnp.where(i == j, 1.0, 0.0).astype(jnp.float32)
    green = jnp.minimum(later, earlier) * (1.0 - jnp.maximum(later, earlier))
    integral = eye + KERNEL_GAIN / 128 * green
    for c in range(3):
        m = jnp.dot(white_ref[0, c], integral, precision=lax.Precision.HIGHEST, preferred_element_type=jnp.float32) * row_scale
        g = jnp.dot(jnp.transpose(m), m, precision=lax.Precision.HIGHEST, preferred_element_type=jnp.float32)
        high = g.astype(jnp.bfloat16)
        low = (g - high.astype(jnp.float32)).astype(jnp.bfloat16)
        mixers[a, c * 128 : (c + 1) * 128, :] = jnp.concatenate([high, low], axis=1)

    counter = [0]
    started = []

    class Link:
        def __init__(self, target, src, landing):
            self.n = counter[0]
            counter[0] += 1
            self.target, self.src, self.landing = target, src, landing

        def start(self):
            self.copy = pltpu.make_async_remote_copy(
                src_ref=self.src, dst_ref=self.src, send_sem=send_sem.at[self.n], recv_sem=recv_sem.at[self.n],
                device_id=self.target, device_id_type=MESH,
            )
            self.copy.start()
            started.append(self.copy)

        def arrived(self):
            pltpu.make_async_remote_copy(
                src_ref=self.landing, dst_ref=self.landing, send_sem=send_sem.at[self.n], recv_sem=recv_sem.at[self.n],
                device_id=self.target, device_id_type=MESH,
            ).wait_recv()

    tasks = {}

    def at(key, act):
        tasks[key] = act

    def row_part(part, dz, half=None):
        same = part != "E1"
        lo, n = (0, EARLY) if part in ("E0", "E1") else (EARLY, 16 - EARLY)
        if half is not None:
            n1 = n // 2
            lo, n = (lo, n1) if half == 0 else (lo + n1, n - n1)
        return rows.at[par_at(same, dz), pl.ds(lo, n)]

    parts = ("L", "E0", "E1")
    z_to = {1: (a, par_at(True, 1)), -1: (a, par_at(True, -1))}
    ring = {}
    for step in range(1, 5):
        for part in parts:
            for d in (1, -1):
                half = None if step < 4 else (0 if d == 1 else 1)
                ring[step, part, d] = Link(
                    z_to[d], row_part(part, -d * (step - 1), half), row_part(part, -d * step, half)
                )
    cross_early = Link(yh_partner, rows.at[p, pl.ds(0, EARLY)], rows.at[par_at(False, 0), pl.ds(0, EARLY)])
    late = pl.ds(EARLY, 16 - EARLY)
    cross_late = {
        dz: Link(yh_partner, rows.at[par_at(True, dz), late], rows.at[par_at(False, dz), late])
        for dz in (0, 1, -1, 2, -2, 3, -3, 4)
    }

    def rows_ready():
        pltpu.make_async_copy(rows.at[p, pl.ds(0, 15)], rows.at[p, pl.ds(0, 15)], bulk_recv.at[0]).wait()
        cross_early.start()
        for part in ("L", "E0"):
            for d in (1, -1):
                ring[1, part, d].start()

    at("rows", rows_ready)

    def early_crossed():
        cross_early.arrived()
        for d in (1, -1):
            ring[1, "E1", d].start()

    at("early", early_crossed)

    def ring_arrival(step, part, d):
        ring[step, part, d].arrived()
        if step < 4:
            ring[step + 1, part, d].start()

    for step in range(1, 5):
        for part in parts:
            for d in (1, -1):
                at(("z", step, part, d), lambda s=step, q=part, d=d: ring_arrival(s, q, d))

    for dz in cross_late:
        at(("late", dz), lambda dz=dz: cross_late[dz].start())

    def gather_over_arc(name, buf, extent, first):
        def piece(arc, half=None):
            if half is None:
                return buf.at[arc]
            n = extent // 2
            return buf.at[arc, pl.ds(half * n, n)]

        x_to = {1: (arc_at(1, True, True), p), -1: (arc_at(-1, True, True), p)}
        to_yl = Link(yl_partner, piece(a), piece(arc_at(0, False, True)))
        hops, cores = {}, {}
        for mine in (True, False):
            for d in (1, -1):
                hops[1, mine, d] = Link(x_to[d], piece(arc_at(0, mine, True)), piece(arc_at(-d, mine, True)))
                half = 0 if d == 1 else 1
                hops[2, mine, d] = Link(x_to[d], piece(arc_at(-d, mine, True), half), piece(arc_at(2, mine, True), half))
            cores[0, mine] = Link(other_core, piece(arc_at(0, mine, True)), piece(arc_at(0, mine, False)))
            for d in (1, -1):
                cores[1, mine, d] = Link(other_core, piece(arc_at(-d, mine, True)), piece(arc_at(-d, mine, False)))
                half = 0 if d == 1 else 1
                cores[2, mine, d] = Link(other_core, piece(arc_at(2, mine, True), half), piece(arc_at(2, mine, False), half))

        def begin():
            first()
            to_yl.start()
            for d in (1, -1):
                hops[1, True, d].start()
            cores[0, True].start()

        def yl_arrival():
            to_yl.arrived()
            for d in (1, -1):
                hops[1, False, d].start()
            cores[0, False].start()

        def hop_arrival(dist, mine, d):
            hops[dist, mine, d].arrived()
            if dist == 1:
                hops[2, mine, d].start()
            cores[dist, mine, d].start()

        at((name, "begin"), begin)
        at((name, "yl"), yl_arrival)
        for mine in (True, False):
            for dist in (1, 2):
                for d in (1, -1):
                    at((name, dist, mine, d), lambda s=dist, m=mine, d=d: hop_arrival(s, m, d))

        def wait_group(dist, mine):
            if dist == 0:
                cores[0, mine].arrived()
            else:
                for d in (1, -1):
                    cores[dist, mine, d].arrived()

        return wait_group

    wait_g = gather_over_arc("G", mixers, 384, lambda: None)

    def cols_ready():
        pltpu.make_async_copy(cols.at[a, pl.ds(0, 15)], cols.at[a, pl.ds(0, 15)], bulk_recv.at[1]).wait()

    wait_c = gather_over_arc("C", cols, 16, cols_ready)

    def mix(arc):
        for c in range(3):
            unit = cols[arc, :, c * 16 : (c + 1) * 16, :].astype(jnp.float32).reshape(16, 2, 8, 256)
            b = jnp.concatenate([unit[:, 0].reshape(128, 256), unit[:, 1].reshape(128, 256)], axis=1).astype(jnp.bfloat16)
            q = jnp.dot(
                mixers[arc, c * 128 : (c + 1) * 128, :], jnp.concatenate([b, b], axis=0), preferred_element_type=jnp.float32
            )
            q = jnp.swapaxes(q.reshape(2, 8, 8, 512), 0, 1).reshape(8, 16, 512)
            high = q.astype(jnp.bfloat16)
            q_high[:, arc * 3 + c] = high
            q_low[:, arc * 3 + c] = (q - high.astype(jnp.float32)).astype(jnp.bfloat16)

    def mix_group(dist, mine):
        wait_g(dist, mine)
        wait_c(dist, mine)
        yl_of = yl if mine else 1 - yl
        if dist == 1:
            def body(k, _):
                dx = (k // 2) * 2 - 1
                mix(((x + dx + 4) % 4) * 4 + yl_of * 2 + k % 2)
                return 0
            lax.fori_loop(0, 4, body, 0)
        else:
            def body(k, _):
                mix(((x + dist) % 4) * 4 + yl_of * 2 + k)
                return 0
            lax.fori_loop(0, 2, body, 0)

    for dist in range(3):
        for mine in (True, False):
            at(("mix", dist, mine), lambda s=dist, m=mine: mix_group(s, m))

    def turn(dz):
        cross_late[dz].arrived()
        at_z = (z + dz + 8) % 8
        halves = []
        for h in range(2):
            sides = [
                rows[side * 8 + at_z].astype(jnp.float32).reshape(16, 3, 2, 8, 256)[:, :, h].reshape(48, 1, 8, 256)
                for side in range(2)
            ]
            halves.append(jnp.concatenate(sides, axis=1).reshape(768, 256))
        rows_t[at_z] = jnp.transpose(jnp.concatenate(halves, axis=1).astype(jnp.bfloat16))

    def clear():
        out_ref[...] = jnp.zeros_like(out_ref)

    at("clear", clear)
    for dz in cross_late:
        at(("turn", dz), lambda dz=dz: turn(dz))

    def accumulate(at_z):
        left = rows_t[at_z]
        right = jnp.concatenate([q_high[at_z].reshape(768, 512), q_low[at_z].reshape(768, 512)], axis=0)
        out_ref[...] += jnp.dot(jnp.concatenate([left, left], axis=1), right, preferred_element_type=jnp.float32)

    def accumulate_group(group):
        first, stride, count = group

        def body(k, _):
            accumulate((z + first + stride * k + 8) % 8)
            return 0

        lax.fori_loop(0, count, body, 0)

    for group in GROUPS:
        at(("sum", group), lambda g=group: accumulate_group(g))

    assert sorted(map(str, tasks)) == sorted(map(str, ORDER))
    for key in ORDER:
        tasks[key]()

    assert counter[0] <= N_SEM
    for n in (0, 1):
        pltpu.make_async_copy(blocks.at[pl.ds(0, 15)], blocks.at[pl.ds(0, 15)], bulk_send.at[n]).wait()
    for copy in started:
        copy.wait_send()


def on_device(partials, epoch_index, whitening):
    vmem = pl.BlockSpec(memory_space=pltpu.VMEM)
    return pl.pallas_call(
        kernel,
        out_shape=jax.ShapeDtypeStruct((512, 512), jnp.float32),
        in_specs=[vmem, vmem, vmem],
        out_specs=vmem,
        scratch_shapes=[
            pltpu.VMEM((16, 48, 256), jnp.bfloat16),
            pltpu.VMEM((16, 16, 48, 256), jnp.bfloat16),
            pltpu.VMEM((16, 16, 48, 256), jnp.bfloat16),
            pltpu.VMEM((16, 384, 256), jnp.bfloat16),
            pltpu.VMEM((8, 512, 768), jnp.bfloat16),
            pltpu.VMEM((8, 48, 16, 512), jnp.bfloat16),
            pltpu.VMEM((8, 48, 16, 512), jnp.bfloat16),
            pltpu.SemaphoreType.DMA((N_SEM,)),
            pltpu.SemaphoreType.DMA((N_SEM,)),
            pltpu.SemaphoreType.DMA((2,)),
            pltpu.SemaphoreType.DMA((2,)),
        ],
        compiler_params=pltpu.CompilerParams(
            collective_id=0, has_side_effects=True, vmem_limit_bytes=56 * 2**20
        ),
    )(partials, epoch_index, whitening)


def solution(mesh):
    placed = (P("arc", None, "par", None), P("arc", None), P("arc", None, None, None))
    return jax.shard_map(
        on_device, mesh=mesh, in_specs=placed, out_specs=P("arc", "par"), check_vma=False
    )
```

```python
import math

import jax
import jax.numpy as jnp
from jax import lax
from jax.experimental import pallas as pl
from jax.experimental.pallas import tpu as pltpu
from jax.sharding import PartitionSpec as P

KERNEL_GAIN = 8.0
MESH = pl.DeviceIdType.MESH
EARLY = 8
N_SEM = 80
GROUPS = ((-2, 1, 5), (-3, 6, 2), (4, 1, 1))
ORDER = (
    "clear", ("G", "begin"), ("G", 1, True, 1), ("G", 1, True, -1), "rows", ("C", "begin"), ("G", 2, True, 1),
    ("G", "yl"), "early", ("z", 1, "L", 1), ("late", 0), ("z", 1, "E0", -1), ("mix", 0, True), ("late", -1),
    ("G", 1, False, 1), ("z", 1, "L", -1), ("late", 1), ("G", 1, False, -1), ("C", 1, True, 1),
    ("z", 1, "E0", 1), ("C", 1, True, -1), ("mix", 1, True), ("G", 2, False, 1), ("G", 2, True, -1),
    ("C", "yl"), ("C", 2, True, -1), ("G", 2, False, -1), ("z", 1, "E1", -1), ("z", 1, "E1", 1),
    ("z", 2, "L", -1), ("late", 2), ("z", 2, "E0", 1), ("turn", 0), ("turn", -1), ("z", 2, "L", 1),
    ("late", -2), ("mix", 0, False), ("C", 2, True, 1), ("turn", 1), ("z", 2, "E0", -1), ("mix", 2, True),
    ("C", 1, False, -1), ("C", 1, False, 1), ("mix", 1, False), ("z", 3, "L", -1), ("late", 3),
    ("z", 3, "E0", 1), ("C", 2, False, 1), ("C", 2, False, -1), ("z", 2, "E1", -1), ("turn", 2),
    ("z", 3, "E0", -1), ("z", 3, "L", 1), ("late", -3), ("z", 2, "E1", 1), ("turn", -2), ("mix", 2, False),
    ("sum", (-2, 1, 5)), ("z", 4, "L", 1), ("z", 4, "L", -1), ("late", 4), ("z", 4, "E0", 1),
    ("z", 3, "E1", -1), ("turn", 3), ("z", 3, "E1", 1), ("turn", -3), ("sum", (-3, 6, 2)), ("z", 4, "E1", 1),
    ("z", 4, "E0", -1), ("z", 4, "E1", -1), ("turn", 4), ("sum", (4, 1, 1)),
)


def kernel(part_hbm, epoch_hbm, white_hbm, out_ref, part_ref, epoch_ref, white_ref, load_sem, blocks, rows, cols, mixers, rows_t, q_high, q_low, send_sem, recv_sem, bulk_send, bulk_recv):
    a = lax.axis_index("arc")
    p = lax.axis_index("par")
    x, yl, core = a // 4, (a // 2) % 2, a % 2
    yh, z = p // 8, p % 8
    other_core = (x * 4 + yl * 2 + 1 - core, p)
    yl_partner = (x * 4 + (1 - yl) * 2 + core, p)
    yh_partner = (a, (1 - yh) * 8 + z)

    def arc_at(dx, same_yl, same_core):
        return (
            ((x + dx + 4) % 4) * 4
            + (yl if same_yl else 1 - yl) * 2
            + (core if same_core else 1 - core)
        )

    def par_at(same_yh, dz):
        return (yh if same_yh else 1 - yh) * 8 + (z + dz + 8) % 8

    barrier = pltpu.get_barrier_semaphore()

    def greet(k, _):
        pl.semaphore_signal(barrier, inc=1, device_id=((a + k) % 16, p), device_id_type=MESH)
        pl.semaphore_signal(barrier, inc=1, device_id=(a, (p + k) % 16), device_id_type=MESH)
        return 0

    lax.fori_loop(1, 16, greet, 0)
    loads = [
        pltpu.make_async_copy(src, dst, load_sem.at[n])
        for n, (src, dst) in enumerate(((part_hbm, part_ref), (epoch_hbm, epoch_ref), (white_hbm, white_ref)))
    ]
    for load in loads:
        load.start()
    loads[0].wait()

    for c in range(3):
        for b in range(16):
            piece = part_ref[0, c, :, b * 512 : (b + 1) * 512].astype(jnp.float32)
            unit = jnp.concatenate([piece[:, :256], piece[:, 256:]], axis=0)
            blocks[b, c * 16 : (c + 1) * 16, :] = unit.astype(jnp.bfloat16)

    pl.semaphore_wait(barrier, 30)

    def send_rows(k, _):
        b = (a + k) % 16
        pltpu.make_async_remote_copy(
            src_ref=blocks.at[b], dst_ref=rows.at[p, a], send_sem=bulk_send.at[0], recv_sem=bulk_recv.at[0],
            device_id=(b, p), device_id_type=MESH,
        ).start()
        return 0

    def send_cols(k, _):
        b = (p + k) % 16
        pltpu.make_async_remote_copy(
            src_ref=blocks.at[b], dst_ref=cols.at[a, p], send_sem=bulk_send.at[1], recv_sem=bulk_recv.at[1],
            device_id=(a, b), device_id_type=MESH,
        ).start()
        return 0

    lax.fori_loop(1, 16, send_rows, 0)
    lax.fori_loop(1, 16, send_cols, 0)
    rows[p, a] = blocks[a]
    cols[a, p] = blocks[p]

    loads[1].wait()
    loads[2].wait()

    row_scale = 1.0 / math.sqrt(6144)
    times = epoch_ref[...].astype(jnp.float32) / jnp.float32(511)
    later = jnp.broadcast_to(times, (128, 128))
    earlier = jnp.transpose(later)
    i = lax.broadcasted_iota(jnp.int32, (128, 128), 0)
    j = lax.broadcasted_iota(jnp.int32, (128, 128), 1)
    eye = jnp.where(i == j, 1.0, 0.0).astype(jnp.float32)
    green = jnp.minimum(later, earlier) * (1.0 - jnp.maximum(later, earlier))
    integral = eye + KERNEL_GAIN / 128 * green
    for c in range(3):
        m = jnp.dot(white_ref[0, c], integral, precision=lax.Precision.HIGHEST, preferred_element_type=jnp.float32) * row_scale
        g = jnp.dot(jnp.transpose(m), m, precision=lax.Precision.HIGHEST, preferred_element_type=jnp.float32)
        high = g.astype(jnp.bfloat16)
        low = (g - high.astype(jnp.float32)).astype(jnp.bfloat16)
        mixers[a, c * 128 : (c + 1) * 128, :] = jnp.concatenate([high, low], axis=1)

    counter = [0]
    started = []

    class Link:
        def __init__(self, target, src, landing):
            self.n = counter[0]
            counter[0] += 1
            self.target, self.src, self.landing = target, src, landing

        def start(self):
            self.copy = pltpu.make_async_remote_copy(
                src_ref=self.src, dst_ref=self.src, send_sem=send_sem.at[self.n], recv_sem=recv_sem.at[self.n],
                device_id=self.target, device_id_type=MESH,
            )
            self.copy.start()
            started.append(self.copy)

        def arrived(self):
            pltpu.make_async_remote_copy(
                src_ref=self.landing, dst_ref=self.landing, send_sem=send_sem.at[self.n], recv_sem=recv_sem.at[self.n],
                device_id=self.target, device_id_type=MESH,
            ).wait_recv()

    tasks = {}

    def at(key, act):
        tasks[key] = act

    def row_part(part, dz, half=None):
        same = part != "E1"
        lo, n = (0, EARLY) if part in ("E0", "E1") else (EARLY, 16 - EARLY)
        if half is not None:
            n1 = n // 2
            lo, n = (lo, n1) if half == 0 else (lo + n1, n - n1)
        return rows.at[par_at(same, dz), pl.ds(lo, n)]

    parts = ("L", "E0", "E1")
    z_to = {1: (a, par_at(True, 1)), -1: (a, par_at(True, -1))}
    ring = {}
    for step in range(1, 5):
        for part in parts:
            for d in (1, -1):
                half = None if step < 4 else (0 if d == 1 else 1)
                ring[step, part, d] = Link(
                    z_to[d], row_part(part, -d * (step - 1), half), row_part(part, -d * step, half)
                )
    cross_early = Link(yh_partner, rows.at[p, pl.ds(0, EARLY)], rows.at[par_at(False, 0), pl.ds(0, EARLY)])
    late = pl.ds(EARLY, 16 - EARLY)
    cross_late = {
        dz: Link(yh_partner, rows.at[par_at(True, dz), late], rows.at[par_at(False, dz), late])
        for dz in (0, 1, -1, 2, -2, 3, -3, 4)
    }

    def rows_ready():
        pltpu.make_async_copy(rows.at[p, pl.ds(0, 15)], rows.at[p, pl.ds(0, 15)], bulk_recv.at[0]).wait()
        cross_early.start()
        for part in ("L", "E0"):
            for d in (1, -1):
                ring[1, part, d].start()

    at("rows", rows_ready)

    def early_crossed():
        cross_early.arrived()
        for d in (1, -1):
            ring[1, "E1", d].start()

    at("early", early_crossed)

    def ring_arrival(step, part, d):
        ring[step, part, d].arrived()
        if step < 4:
            ring[step + 1, part, d].start()

    for step in range(1, 5):
        for part in parts:
            for d in (1, -1):
                at(("z", step, part, d), lambda s=step, q=part, d=d: ring_arrival(s, q, d))

    for dz in cross_late:
        at(("late", dz), lambda dz=dz: cross_late[dz].start())

    def gather_over_arc(name, buf, extent, first):
        def piece(arc, half=None):
            if half is None:
                return buf.at[arc]
            n = extent // 2
            return buf.at[arc, pl.ds(half * n, n)]

        x_to = {1: (arc_at(1, True, True), p), -1: (arc_at(-1, True, True), p)}
        to_yl = Link(yl_partner, piece(a), piece(arc_at(0, False, True)))
        hops, cores = {}, {}
        for mine in (True, False):
            for d in (1, -1):
                hops[1, mine, d] = Link(x_to[d], piece(arc_at(0, mine, True)), piece(arc_at(-d, mine, True)))
                half = 0 if d == 1 else 1
                hops[2, mine, d] = Link(x_to[d], piece(arc_at(-d, mine, True), half), piece(arc_at(2, mine, True), half))
            cores[0, mine] = Link(other_core, piece(arc_at(0, mine, True)), piece(arc_at(0, mine, False)))
            for d in (1, -1):
                cores[1, mine, d] = Link(other_core, piece(arc_at(-d, mine, True)), piece(arc_at(-d, mine, False)))
                half = 0 if d == 1 else 1
                cores[2, mine, d] = Link(other_core, piece(arc_at(2, mine, True), half), piece(arc_at(2, mine, False), half))

        def begin():
            first()
            to_yl.start()
            for d in (1, -1):
                hops[1, True, d].start()
            cores[0, True].start()

        def yl_arrival():
            to_yl.arrived()
            for d in (1, -1):
                hops[1, False, d].start()
            cores[0, False].start()

        def hop_arrival(dist, mine, d):
            hops[dist, mine, d].arrived()
            if dist == 1:
                hops[2, mine, d].start()
            cores[dist, mine, d].start()

        at((name, "begin"), begin)
        at((name, "yl"), yl_arrival)
        for mine in (True, False):
            for dist in (1, 2):
                for d in (1, -1):
                    at((name, dist, mine, d), lambda s=dist, m=mine, d=d: hop_arrival(s, m, d))

        def wait_group(dist, mine):
            if dist == 0:
                cores[0, mine].arrived()
            else:
                for d in (1, -1):
                    cores[dist, mine, d].arrived()

        return wait_group

    wait_g = gather_over_arc("G", mixers, 384, lambda: None)

    def cols_ready():
        pltpu.make_async_copy(cols.at[a, pl.ds(0, 15)], cols.at[a, pl.ds(0, 15)], bulk_recv.at[1]).wait()

    wait_c = gather_over_arc("C", cols, 16, cols_ready)

    def mix(arc):
        for c in range(3):
            unit = cols[arc, :, c * 16 : (c + 1) * 16, :].astype(jnp.float32).reshape(16, 2, 8, 256)
            b = jnp.concatenate([unit[:, 0].reshape(128, 256), unit[:, 1].reshape(128, 256)], axis=1).astype(jnp.bfloat16)
            q = jnp.dot(
                mixers[arc, c * 128 : (c + 1) * 128, :], jnp.concatenate([b, b], axis=0), preferred_element_type=jnp.float32
            )
            q = jnp.swapaxes(q.reshape(2, 8, 8, 512), 0, 1).reshape(8, 16, 512)
            high = q.astype(jnp.bfloat16)
            q_high[:, arc * 3 + c] = high
            q_low[:, arc * 3 + c] = (q - high.astype(jnp.float32)).astype(jnp.bfloat16)

    def mix_group(dist, mine):
        wait_g(dist, mine)
        wait_c(dist, mine)
        yl_of = yl if mine else 1 - yl
        if dist == 1:
            def body(k, _):
                dx = (k // 2) * 2 - 1
                mix(((x + dx + 4) % 4) * 4 + yl_of * 2 + k % 2)
                return 0
            lax.fori_loop(0, 4, body, 0)
        else:
            def body(k, _):
                mix(((x + dist) % 4) * 4 + yl_of * 2 + k)
                return 0
            lax.fori_loop(0, 2, body, 0)

    for dist in range(3):
        for mine in (True, False):
            at(("mix", dist, mine), lambda s=dist, m=mine: mix_group(s, m))

    def turn(dz):
        cross_late[dz].arrived()
        at_z = (z + dz + 8) % 8
        halves = []
        for h in range(2):
            sides = [
                rows[side * 8 + at_z].astype(jnp.float32).reshape(16, 3, 2, 8, 256)[:, :, h].reshape(48, 1, 8, 256)
                for side in range(2)
            ]
            halves.append(jnp.concatenate(sides, axis=1).reshape(768, 256))
        rows_t[at_z] = jnp.transpose(jnp.concatenate(halves, axis=1).astype(jnp.bfloat16))

    def clear():
        out_ref[...] = jnp.zeros_like(out_ref)

    at("clear", clear)
    for dz in cross_late:
        at(("turn", dz), lambda dz=dz: turn(dz))

    def accumulate(at_z):
        left = rows_t[at_z]
        right = jnp.concatenate([q_high[at_z].reshape(768, 512), q_low[at_z].reshape(768, 512)], axis=0)
        out_ref[...] += jnp.dot(jnp.concatenate([left, left], axis=1), right, preferred_element_type=jnp.float32)

    def accumulate_group(group):
        first, stride, count = group

        def body(k, _):
            accumulate((z + first + stride * k + 8) % 8)
            return 0

        lax.fori_loop(0, count, body, 0)

    for group in GROUPS:
        at(("sum", group), lambda g=group: accumulate_group(g))

    assert sorted(map(str, tasks)) == sorted(map(str, ORDER))
    for key in ORDER:
        tasks[key]()

    assert counter[0] <= N_SEM
    for n in (0, 1):
        pltpu.make_async_copy(blocks.at[pl.ds(0, 15)], blocks.at[pl.ds(0, 15)], bulk_send.at[n]).wait()
    for copy in started:
        copy.wait_send()


def on_device(partials, epoch_index, whitening):
    vmem = pl.BlockSpec(memory_space=pltpu.VMEM)
    return pl.pallas_call(
        kernel,
        out_shape=jax.ShapeDtypeStruct((512, 512), jnp.float32),
        in_specs=[pl.BlockSpec(memory_space=pl.ANY)] * 3,
        out_specs=vmem,
        scratch_shapes=[
            pltpu.VMEM((1, 3, 8, 8192), jnp.bfloat16),
            pltpu.VMEM((1, 128), jnp.int32),
            pltpu.VMEM((1, 3, 128, 128), jnp.float32),
            pltpu.SemaphoreType.DMA((3,)),
            pltpu.VMEM((16, 48, 256), jnp.bfloat16),
            pltpu.VMEM((16, 16, 48, 256), jnp.bfloat16),
            pltpu.VMEM((16, 16, 48, 256), jnp.bfloat16),
            pltpu.VMEM((16, 384, 256), jnp.bfloat16),
            pltpu.VMEM((8, 512, 768), jnp.bfloat16),
            pltpu.VMEM((8, 48, 16, 512), jnp.bfloat16),
            pltpu.VMEM((8, 48, 16, 512), jnp.bfloat16),
            pltpu.SemaphoreType.DMA((N_SEM,)),
            pltpu.SemaphoreType.DMA((N_SEM,)),
            pltpu.SemaphoreType.DMA((2,)),
            pltpu.SemaphoreType.DMA((2,)),
        ],
        compiler_params=pltpu.CompilerParams(
            collective_id=0, has_side_effects=True, vmem_limit_bytes=56 * 2**20
        ),
    )(partials, epoch_index, whitening)


def solution(mesh):
    placed = (P("arc", None, "par", None), P("arc", None), P("arc", None, None, None))
    return jax.shard_map(
        on_device, mesh=mesh, in_specs=placed, out_specs=P("arc", "par"), check_vma=False
    )
```

```python
import math

import jax
import jax.numpy as jnp
from jax import lax
from jax.experimental import pallas as pl
from jax.experimental.pallas import tpu as pltpu
from jax.sharding import PartitionSpec as P

KERNEL_GAIN = 8.0
MESH = pl.DeviceIdType.MESH
EARLY = 9
N_SEM = 80
GROUPS = ((-2, 1, 5), (-3, 6, 2), (4, 1, 1))
ORDER = (
    "clear", ("G", "begin"), ("G", 1, True, 1), ("G", 1, True, -1), "rows", ("C", "begin"), ("G", 2, True, 1),
    ("G", "yl"), "early", ("z", 1, "L", 1), ("late", 0), ("z", 1, "E0", -1), ("mix", 0, True), ("late", -1),
    ("G", 1, False, 1), ("z", 1, "L", -1), ("late", 1), ("G", 1, False, -1), ("C", 1, True, 1),
    ("z", 1, "E0", 1), ("C", 1, True, -1), ("mix", 1, True), ("G", 2, False, 1), ("G", 2, True, -1),
    ("C", "yl"), ("C", 2, True, -1), ("G", 2, False, -1), ("z", 1, "E1", -1), ("z", 1, "E1", 1),
    ("z", 2, "L", -1), ("late", 2), ("z", 2, "E0", 1), ("turn", 0), ("turn", -1), ("z", 2, "L", 1),
    ("late", -2), ("mix", 0, False), ("C", 2, True, 1), ("turn", 1), ("z", 2, "E0", -1), ("mix", 2, True),
    ("C", 1, False, -1), ("C", 1, False, 1), ("mix", 1, False), ("z", 3, "L", -1), ("late", 3),
    ("z", 3, "E0", 1), ("C", 2, False, 1), ("C", 2, False, -1), ("z", 2, "E1", -1), ("turn", 2),
    ("z", 3, "E0", -1), ("z", 3, "L", 1), ("late", -3), ("z", 2, "E1", 1), ("turn", -2), ("mix", 2, False),
    ("sum", (-2, 1, 5)), ("z", 4, "L", 1), ("z", 4, "L", -1), ("late", 4), ("z", 4, "E0", 1),
    ("z", 3, "E1", -1), ("turn", 3), ("z", 3, "E1", 1), ("turn", -3), ("sum", (-3, 6, 2)), ("z", 4, "E1", 1),
    ("z", 4, "E0", -1), ("z", 4, "E1", -1), ("turn", 4), ("sum", (4, 1, 1)),
)


def kernel(part_hbm, epoch_hbm, white_hbm, out_ref, part_ref, epoch_ref, white_ref, load_sem, blocks, rows, cols, mixers, rows_t, q_high, q_low, send_sem, recv_sem, bulk_send, bulk_recv):
    a = lax.axis_index("arc")
    p = lax.axis_index("par")
    x, yl, core = a // 4, (a // 2) % 2, a % 2
    yh, z = p // 8, p % 8
    other_core = (x * 4 + yl * 2 + 1 - core, p)
    yl_partner = (x * 4 + (1 - yl) * 2 + core, p)
    yh_partner = (a, (1 - yh) * 8 + z)

    def arc_at(dx, same_yl, same_core):
        return (
            ((x + dx + 4) % 4) * 4
            + (yl if same_yl else 1 - yl) * 2
            + (core if same_core else 1 - core)
        )

    def par_at(same_yh, dz):
        return (yh if same_yh else 1 - yh) * 8 + (z + dz + 8) % 8

    barrier = pltpu.get_barrier_semaphore()

    def greet(k, _):
        pl.semaphore_signal(barrier, inc=1, device_id=((a + k) % 16, p), device_id_type=MESH)
        pl.semaphore_signal(barrier, inc=1, device_id=(a, (p + k) % 16), device_id_type=MESH)
        return 0

    lax.fori_loop(1, 16, greet, 0)
    loads = [
        pltpu.make_async_copy(src, dst, load_sem.at[n])
        for n, (src, dst) in enumerate(((part_hbm, part_ref), (epoch_hbm, epoch_ref), (white_hbm, white_ref)))
    ]
    for load in loads:
        load.start()
    loads[0].wait()

    for c in range(3):
        for b in range(16):
            piece = part_ref[0, c, :, b * 512 : (b + 1) * 512].astype(jnp.float32)
            unit = jnp.concatenate([piece[:, :256], piece[:, 256:]], axis=0)
            blocks[b, c * 16 : (c + 1) * 16, :] = unit.astype(jnp.bfloat16)

    pl.semaphore_wait(barrier, 30)

    def send_rows(k, _):
        b = (a + k) % 16
        pltpu.make_async_remote_copy(
            src_ref=blocks.at[b], dst_ref=rows.at[p, a], send_sem=bulk_send.at[0], recv_sem=bulk_recv.at[0],
            device_id=(b, p), device_id_type=MESH,
        ).start()
        return 0

    def send_cols(k, _):
        b = (p + k) % 16
        pltpu.make_async_remote_copy(
            src_ref=blocks.at[b], dst_ref=cols.at[a, p], send_sem=bulk_send.at[1], recv_sem=bulk_recv.at[1],
            device_id=(a, b), device_id_type=MESH,
        ).start()
        return 0

    lax.fori_loop(1, 16, send_rows, 0)
    lax.fori_loop(1, 16, send_cols, 0)
    rows[p, a] = blocks[a]
    cols[a, p] = blocks[p]

    loads[1].wait()
    loads[2].wait()

    row_scale = 1.0 / math.sqrt(6144)
    times = epoch_ref[...].astype(jnp.float32) / jnp.float32(511)
    later = jnp.broadcast_to(times, (128, 128))
    earlier = jnp.transpose(later)
    i = lax.broadcasted_iota(jnp.int32, (128, 128), 0)
    j = lax.broadcasted_iota(jnp.int32, (128, 128), 1)
    eye = jnp.where(i == j, 1.0, 0.0).astype(jnp.float32)
    green = jnp.minimum(later, earlier) * (1.0 - jnp.maximum(later, earlier))
    integral = eye + KERNEL_GAIN / 128 * green
    for c in range(3):
        m = jnp.dot(white_ref[0, c], integral, precision=lax.Precision.HIGHEST, preferred_element_type=jnp.float32) * row_scale
        g = jnp.dot(jnp.transpose(m), m, precision=lax.Precision.HIGHEST, preferred_element_type=jnp.float32)
        high = g.astype(jnp.bfloat16)
        low = (g - high.astype(jnp.float32)).astype(jnp.bfloat16)
        mixers[a, c * 128 : (c + 1) * 128, :] = jnp.concatenate([high, low], axis=1)

    counter = [0]
    started = []

    class Link:
        def __init__(self, target, src, landing):
            self.n = counter[0]
            counter[0] += 1
            self.target, self.src, self.landing = target, src, landing

        def start(self):
            self.copy = pltpu.make_async_remote_copy(
                src_ref=self.src, dst_ref=self.src, send_sem=send_sem.at[self.n], recv_sem=recv_sem.at[self.n],
                device_id=self.target, device_id_type=MESH,
            )
            self.copy.start()
            started.append(self.copy)

        def arrived(self):
            pltpu.make_async_remote_copy(
                src_ref=self.landing, dst_ref=self.landing, send_sem=send_sem.at[self.n], recv_sem=recv_sem.at[self.n],
                device_id=self.target, device_id_type=MESH,
            ).wait_recv()

    tasks = {}

    def at(key, act):
        tasks[key] = act

    def row_part(part, dz, half=None):
        same = part != "E1"
        lo, n = (0, EARLY) if part in ("E0", "E1") else (EARLY, 16 - EARLY)
        if half is not None:
            n1 = n // 2
            lo, n = (lo, n1) if half == 0 else (lo + n1, n - n1)
        return rows.at[par_at(same, dz), pl.ds(lo, n)]

    parts = ("L", "E0", "E1")
    z_to = {1: (a, par_at(True, 1)), -1: (a, par_at(True, -1))}
    ring = {}
    for step in range(1, 5):
        for part in parts:
            for d in (1, -1):
                half = None if step < 4 else (0 if d == 1 else 1)
                ring[step, part, d] = Link(
                    z_to[d], row_part(part, -d * (step - 1), half), row_part(part, -d * step, half)
                )
    cross_early = Link(yh_partner, rows.at[p, pl.ds(0, EARLY)], rows.at[par_at(False, 0), pl.ds(0, EARLY)])
    late = pl.ds(EARLY, 16 - EARLY)
    cross_late = {
        dz: Link(yh_partner, rows.at[par_at(True, dz), late], rows.at[par_at(False, dz), late])
        for dz in (0, 1, -1, 2, -2, 3, -3, 4)
    }

    def rows_ready():
        pltpu.make_async_copy(rows.at[p, pl.ds(0, 15)], rows.at[p, pl.ds(0, 15)], bulk_recv.at[0]).wait()
        cross_early.start()
        for part in ("L", "E0"):
            for d in (1, -1):
                ring[1, part, d].start()

    at("rows", rows_ready)

    def early_crossed():
        cross_early.arrived()
        for d in (1, -1):
            ring[1, "E1", d].start()

    at("early", early_crossed)

    def ring_arrival(step, part, d):
        ring[step, part, d].arrived()
        if step < 4:
            ring[step + 1, part, d].start()

    for step in range(1, 5):
        for part in parts:
            for d in (1, -1):
                at(("z", step, part, d), lambda s=step, q=part, d=d: ring_arrival(s, q, d))

    for dz in cross_late:
        at(("late", dz), lambda dz=dz: cross_late[dz].start())

    def gather_over_arc(name, buf, extent, first):
        def piece(arc, half=None):
            if half is None:
                return buf.at[arc]
            n = extent // 2
            return buf.at[arc, pl.ds(half * n, n)]

        x_to = {1: (arc_at(1, True, True), p), -1: (arc_at(-1, True, True), p)}
        to_yl = Link(yl_partner, piece(a), piece(arc_at(0, False, True)))
        hops, cores = {}, {}
        for mine in (True, False):
            for d in (1, -1):
                hops[1, mine, d] = Link(x_to[d], piece(arc_at(0, mine, True)), piece(arc_at(-d, mine, True)))
                half = 0 if d == 1 else 1
                hops[2, mine, d] = Link(x_to[d], piece(arc_at(-d, mine, True), half), piece(arc_at(2, mine, True), half))
            cores[0, mine] = Link(other_core, piece(arc_at(0, mine, True)), piece(arc_at(0, mine, False)))
            for d in (1, -1):
                cores[1, mine, d] = Link(other_core, piece(arc_at(-d, mine, True)), piece(arc_at(-d, mine, False)))
                half = 0 if d == 1 else 1
                cores[2, mine, d] = Link(other_core, piece(arc_at(2, mine, True), half), piece(arc_at(2, mine, False), half))

        def begin():
            first()
            to_yl.start()
            for d in (1, -1):
                hops[1, True, d].start()
            cores[0, True].start()

        def yl_arrival():
            to_yl.arrived()
            for d in (1, -1):
                hops[1, False, d].start()
            cores[0, False].start()

        def hop_arrival(dist, mine, d):
            hops[dist, mine, d].arrived()
            if dist == 1:
                hops[2, mine, d].start()
            cores[dist, mine, d].start()

        at((name, "begin"), begin)
        at((name, "yl"), yl_arrival)
        for mine in (True, False):
            for dist in (1, 2):
                for d in (1, -1):
                    at((name, dist, mine, d), lambda s=dist, m=mine, d=d: hop_arrival(s, m, d))

        def wait_group(dist, mine):
            if dist == 0:
                cores[0, mine].arrived()
            else:
                for d in (1, -1):
                    cores[dist, mine, d].arrived()

        return wait_group

    wait_g = gather_over_arc("G", mixers, 384, lambda: None)

    def cols_ready():
        pltpu.make_async_copy(cols.at[a, pl.ds(0, 15)], cols.at[a, pl.ds(0, 15)], bulk_recv.at[1]).wait()

    wait_c = gather_over_arc("C", cols, 16, cols_ready)

    def mix(arc):
        for c in range(3):
            unit = cols[arc, :, c * 16 : (c + 1) * 16, :].astype(jnp.float32).reshape(16, 2, 8, 256)
            b = jnp.concatenate([unit[:, 0].reshape(128, 256), unit[:, 1].reshape(128, 256)], axis=1).astype(jnp.bfloat16)
            q = jnp.dot(
                mixers[arc, c * 128 : (c + 1) * 128, :], jnp.concatenate([b, b], axis=0), preferred_element_type=jnp.float32
            )
            q = jnp.swapaxes(q.reshape(2, 8, 8, 512), 0, 1).reshape(8, 16, 512)
            high = q.astype(jnp.bfloat16)
            q_high[:, arc * 3 + c] = high
            q_low[:, arc * 3 + c] = (q - high.astype(jnp.float32)).astype(jnp.bfloat16)

    def mix_group(dist, mine):
        wait_g(dist, mine)
        wait_c(dist, mine)
        yl_of = yl if mine else 1 - yl
        if dist == 1:
            def body(k, _):
                dx = (k // 2) * 2 - 1
                mix(((x + dx + 4) % 4) * 4 + yl_of * 2 + k % 2)
                return 0
            lax.fori_loop(0, 4, body, 0)
        else:
            def body(k, _):
                mix(((x + dist) % 4) * 4 + yl_of * 2 + k)
                return 0
            lax.fori_loop(0, 2, body, 0)

    for dist in range(3):
        for mine in (True, False):
            at(("mix", dist, mine), lambda s=dist, m=mine: mix_group(s, m))

    def turn(dz):
        cross_late[dz].arrived()
        at_z = (z + dz + 8) % 8
        halves = []
        for h in range(2):
            sides = [
                rows[side * 8 + at_z].astype(jnp.float32).reshape(16, 3, 2, 8, 256)[:, :, h].reshape(48, 1, 8, 256)
                for side in range(2)
            ]
            halves.append(jnp.concatenate(sides, axis=1).reshape(768, 256))
        rows_t[at_z] = jnp.transpose(jnp.concatenate(halves, axis=1).astype(jnp.bfloat16))

    def clear():
        out_ref[...] = jnp.zeros_like(out_ref)

    at("clear", clear)
    for dz in cross_late:
        at(("turn", dz), lambda dz=dz: turn(dz))

    def accumulate(at_z):
        left = rows_t[at_z]
        right = jnp.concatenate([q_high[at_z].reshape(768, 512), q_low[at_z].reshape(768, 512)], axis=0)
        out_ref[...] += jnp.dot(jnp.concatenate([left, left], axis=1), right, preferred_element_type=jnp.float32)

    def accumulate_group(group):
        first, stride, count = group

        def body(k, _):
            accumulate((z + first + stride * k + 8) % 8)
            return 0

        lax.fori_loop(0, count, body, 0)

    for group in GROUPS:
        at(("sum", group), lambda g=group: accumulate_group(g))

    assert sorted(map(str, tasks)) == sorted(map(str, ORDER))
    for key in ORDER:
        tasks[key]()

    assert counter[0] <= N_SEM
    for n in (0, 1):
        pltpu.make_async_copy(blocks.at[pl.ds(0, 15)], blocks.at[pl.ds(0, 15)], bulk_send.at[n]).wait()
    for copy in started:
        copy.wait_send()


def on_device(partials, epoch_index, whitening):
    vmem = pl.BlockSpec(memory_space=pltpu.VMEM)
    return pl.pallas_call(
        kernel,
        out_shape=jax.ShapeDtypeStruct((512, 512), jnp.float32),
        in_specs=[pl.BlockSpec(memory_space=pl.ANY)] * 3,
        out_specs=vmem,
        scratch_shapes=[
            pltpu.VMEM((1, 3, 8, 8192), jnp.bfloat16),
            pltpu.VMEM((1, 128), jnp.int32),
            pltpu.VMEM((1, 3, 128, 128), jnp.float32),
            pltpu.SemaphoreType.DMA((3,)),
            pltpu.VMEM((16, 48, 256), jnp.bfloat16),
            pltpu.VMEM((16, 16, 48, 256), jnp.bfloat16),
            pltpu.VMEM((16, 16, 48, 256), jnp.bfloat16),
            pltpu.VMEM((16, 384, 256), jnp.bfloat16),
            pltpu.VMEM((8, 512, 768), jnp.bfloat16),
            pltpu.VMEM((8, 48, 16, 512), jnp.bfloat16),
            pltpu.VMEM((8, 48, 16, 512), jnp.bfloat16),
            pltpu.SemaphoreType.DMA((N_SEM,)),
            pltpu.SemaphoreType.DMA((N_SEM,)),
            pltpu.SemaphoreType.DMA((2,)),
            pltpu.SemaphoreType.DMA((2,)),
        ],
        compiler_params=pltpu.CompilerParams(
            collective_id=0, has_side_effects=True, vmem_limit_bytes=56 * 2**20
        ),
    )(partials, epoch_index, whitening)


def solution(mesh):
    placed = (P("arc", None, "par", None), P("arc", None), P("arc", None, None, None))
    return jax.shard_map(
        on_device, mesh=mesh, in_specs=placed, out_specs=P("arc", "par"), check_vma=False
    )
```

```python
import math

import jax
import jax.numpy as jnp
from jax import lax
from jax.experimental import pallas as pl
from jax.experimental.pallas import tpu as pltpu
from jax.sharding import PartitionSpec as P

KERNEL_GAIN = 8.0
MESH = pl.DeviceIdType.MESH
EARLY = 9
N_SEM = 80
GROUPS = ((-1, 1, 3), (-2, 4, 2), (-3, 6, 2), (4, 1, 1))
ORDER = (
    "clear", ("G", "begin"), ("G", 1, True, 1), ("G", 1, True, -1), "rows", ("C", "begin"), ("G", 2, True, 1),
    ("G", "yl"), "early", ("z", 1, "L", 1), ("late", 0), ("z", 1, "E0", -1), ("mix", 0, True), ("late", -1),
    ("G", 1, False, 1), ("z", 1, "L", -1), ("late", 1), ("G", 1, False, -1), ("C", 1, True, 1),
    ("z", 1, "E0", 1), ("C", 1, True, -1), ("mix", 1, True), ("G", 2, False, 1), ("G", 2, True, -1),
    ("C", "yl"), ("C", 2, True, -1), ("G", 2, False, -1), ("z", 1, "E1", -1), ("z", 1, "E1", 1),
    ("z", 2, "L", -1), ("late", 2), ("z", 2, "E0", 1), ("turn", 0), ("turn", -1), ("z", 2, "L", 1),
    ("late", -2), ("mix", 0, False), ("C", 2, True, 1), ("turn", 1), ("z", 2, "E0", -1), ("mix", 2, True),
    ("C", 1, False, -1), ("C", 1, False, 1), ("mix", 1, False), ("z", 3, "L", -1), ("late", 3),
    ("z", 3, "E0", 1), ("C", 2, False, 1), ("C", 2, False, -1), ("z", 2, "E1", -1), ("turn", 2),
    ("z", 3, "E0", -1), ("z", 3, "L", 1), ("late", -3), ("z", 2, "E1", 1), ("turn", -2), ("mix", 2, False),
    ("sum", (-1, 1, 3)), ("z", 4, "L", 1), ("z", 4, "L", -1), ("late", 4), ("z", 3, "E1", -1),
    ("z", 3, "E1", 1), ("sum", (-2, 4, 2)), ("turn", 3), ("turn", -3), ("z", 4, "E0", 1), ("z", 4, "E0", -1),
    ("sum", (-3, 6, 2)), ("z", 4, "E1", 1), ("z", 4, "E1", -1), ("turn", 4), ("sum", (4, 1, 1)),
)


def kernel(part_hbm, epoch_hbm, white_hbm, out_ref, part_ref, epoch_ref, white_ref, load_sem, blocks, rows, cols, mixers, rows_t, q_high, q_low, send_sem, recv_sem, bulk_send, bulk_recv):
    a = lax.axis_index("arc")
    p = lax.axis_index("par")
    x, yl, core = a // 4, (a // 2) % 2, a % 2
    yh, z = p // 8, p % 8
    other_core = (x * 4 + yl * 2 + 1 - core, p)
    yl_partner = (x * 4 + (1 - yl) * 2 + core, p)
    yh_partner = (a, (1 - yh) * 8 + z)

    def arc_at(dx, same_yl, same_core):
        return (
            ((x + dx + 4) % 4) * 4
            + (yl if same_yl else 1 - yl) * 2
            + (core if same_core else 1 - core)
        )

    def par_at(same_yh, dz):
        return (yh if same_yh else 1 - yh) * 8 + (z + dz + 8) % 8

    barrier = pltpu.get_barrier_semaphore()

    def greet(k, _):
        pl.semaphore_signal(barrier, inc=1, device_id=((a + k) % 16, p), device_id_type=MESH)
        pl.semaphore_signal(barrier, inc=1, device_id=(a, (p + k) % 16), device_id_type=MESH)
        return 0

    lax.fori_loop(1, 16, greet, 0)
    loads = [
        pltpu.make_async_copy(src, dst, load_sem.at[n])
        for n, (src, dst) in enumerate(((part_hbm, part_ref), (epoch_hbm, epoch_ref), (white_hbm, white_ref)))
    ]
    for load in loads:
        load.start()
    loads[0].wait()

    for c in range(3):
        for b in range(16):
            piece = part_ref[0, c, :, b * 512 : (b + 1) * 512].astype(jnp.float32)
            unit = jnp.concatenate([piece[:, :256], piece[:, 256:]], axis=0)
            blocks[b, c * 16 : (c + 1) * 16, :] = unit.astype(jnp.bfloat16)

    pl.semaphore_wait(barrier, 30)

    def send_rows(k, _):
        b = (a + k) % 16
        pltpu.make_async_remote_copy(
            src_ref=blocks.at[b], dst_ref=rows.at[p, a], send_sem=bulk_send.at[0], recv_sem=bulk_recv.at[0],
            device_id=(b, p), device_id_type=MESH,
        ).start()
        return 0

    def send_cols(k, _):
        b = (p + k) % 16
        pltpu.make_async_remote_copy(
            src_ref=blocks.at[b], dst_ref=cols.at[a, p], send_sem=bulk_send.at[1], recv_sem=bulk_recv.at[1],
            device_id=(a, b), device_id_type=MESH,
        ).start()
        return 0

    lax.fori_loop(1, 16, send_rows, 0)
    lax.fori_loop(1, 16, send_cols, 0)
    rows[p, a] = blocks[a]
    cols[a, p] = blocks[p]

    loads[1].wait()
    loads[2].wait()

    row_scale = 1.0 / math.sqrt(6144)
    times = epoch_ref[...].astype(jnp.float32) / jnp.float32(511)
    later = jnp.broadcast_to(times, (128, 128))
    earlier = jnp.transpose(later)
    i = lax.broadcasted_iota(jnp.int32, (128, 128), 0)
    j = lax.broadcasted_iota(jnp.int32, (128, 128), 1)
    eye = jnp.where(i == j, 1.0, 0.0).astype(jnp.float32)
    green = jnp.minimum(later, earlier) * (1.0 - jnp.maximum(later, earlier))
    integral = eye + KERNEL_GAIN / 128 * green
    for c in range(3):
        m = jnp.dot(white_ref[0, c], integral, precision=lax.Precision.HIGHEST, preferred_element_type=jnp.float32) * row_scale
        g = jnp.dot(jnp.transpose(m), m, precision=lax.Precision.HIGHEST, preferred_element_type=jnp.float32)
        high = g.astype(jnp.bfloat16)
        low = (g - high.astype(jnp.float32)).astype(jnp.bfloat16)
        mixers[a, c * 128 : (c + 1) * 128, :] = jnp.concatenate([high, low], axis=1)

    counter = [0]
    started = []

    class Link:
        def __init__(self, target, src, landing):
            self.n = counter[0]
            counter[0] += 1
            self.target, self.src, self.landing = target, src, landing

        def start(self):
            self.copy = pltpu.make_async_remote_copy(
                src_ref=self.src, dst_ref=self.src, send_sem=send_sem.at[self.n], recv_sem=recv_sem.at[self.n],
                device_id=self.target, device_id_type=MESH,
            )
            self.copy.start()
            started.append(self.copy)

        def arrived(self):
            pltpu.make_async_remote_copy(
                src_ref=self.landing, dst_ref=self.landing, send_sem=send_sem.at[self.n], recv_sem=recv_sem.at[self.n],
                device_id=self.target, device_id_type=MESH,
            ).wait_recv()

    tasks = {}

    def at(key, act):
        tasks[key] = act

    def row_part(part, dz, half=None):
        same = part != "E1"
        lo, n = (0, EARLY) if part in ("E0", "E1") else (EARLY, 16 - EARLY)
        if half is not None:
            n1 = n // 2
            lo, n = (lo, n1) if half == 0 else (lo + n1, n - n1)
        return rows.at[par_at(same, dz), pl.ds(lo, n)]

    parts = ("L", "E0", "E1")
    z_to = {1: (a, par_at(True, 1)), -1: (a, par_at(True, -1))}
    ring = {}
    for step in range(1, 5):
        for part in parts:
            for d in (1, -1):
                half = None if step < 4 else (0 if d == 1 else 1)
                ring[step, part, d] = Link(
                    z_to[d], row_part(part, -d * (step - 1), half), row_part(part, -d * step, half)
                )
    cross_early = Link(yh_partner, rows.at[p, pl.ds(0, EARLY)], rows.at[par_at(False, 0), pl.ds(0, EARLY)])
    late = pl.ds(EARLY, 16 - EARLY)
    cross_late = {
        dz: Link(yh_partner, rows.at[par_at(True, dz), late], rows.at[par_at(False, dz), late])
        for dz in (0, 1, -1, 2, -2, 3, -3, 4)
    }

    def rows_ready():
        pltpu.make_async_copy(rows.at[p, pl.ds(0, 15)], rows.at[p, pl.ds(0, 15)], bulk_recv.at[0]).wait()
        cross_early.start()
        for part in ("L", "E0"):
            for d in (1, -1):
                ring[1, part, d].start()

    at("rows", rows_ready)

    def early_crossed():
        cross_early.arrived()
        for d in (1, -1):
            ring[1, "E1", d].start()

    at("early", early_crossed)

    def ring_arrival(step, part, d):
        ring[step, part, d].arrived()
        if step < 4:
            ring[step + 1, part, d].start()

    for step in range(1, 5):
        for part in parts:
            for d in (1, -1):
                at(("z", step, part, d), lambda s=step, q=part, d=d: ring_arrival(s, q, d))

    for dz in cross_late:
        at(("late", dz), lambda dz=dz: cross_late[dz].start())

    def gather_over_arc(name, buf, extent, first):
        def piece(arc, half=None):
            if half is None:
                return buf.at[arc]
            n = extent // 2
            return buf.at[arc, pl.ds(half * n, n)]

        x_to = {1: (arc_at(1, True, True), p), -1: (arc_at(-1, True, True), p)}
        to_yl = Link(yl_partner, piece(a), piece(arc_at(0, False, True)))
        hops, cores = {}, {}
        for mine in (True, False):
            for d in (1, -1):
                hops[1, mine, d] = Link(x_to[d], piece(arc_at(0, mine, True)), piece(arc_at(-d, mine, True)))
                half = 0 if d == 1 else 1
                hops[2, mine, d] = Link(x_to[d], piece(arc_at(-d, mine, True), half), piece(arc_at(2, mine, True), half))
            cores[0, mine] = Link(other_core, piece(arc_at(0, mine, True)), piece(arc_at(0, mine, False)))
            for d in (1, -1):
                cores[1, mine, d] = Link(other_core, piece(arc_at(-d, mine, True)), piece(arc_at(-d, mine, False)))
                half = 0 if d == 1 else 1
                cores[2, mine, d] = Link(other_core, piece(arc_at(2, mine, True), half), piece(arc_at(2, mine, False), half))

        def begin():
            first()
            to_yl.start()
            for d in (1, -1):
                hops[1, True, d].start()
            cores[0, True].start()

        def yl_arrival():
            to_yl.arrived()
            for d in (1, -1):
                hops[1, False, d].start()
            cores[0, False].start()

        def hop_arrival(dist, mine, d):
            hops[dist, mine, d].arrived()
            if dist == 1:
                hops[2, mine, d].start()
            cores[dist, mine, d].start()

        at((name, "begin"), begin)
        at((name, "yl"), yl_arrival)
        for mine in (True, False):
            for dist in (1, 2):
                for d in (1, -1):
                    at((name, dist, mine, d), lambda s=dist, m=mine, d=d: hop_arrival(s, m, d))

        def wait_group(dist, mine):
            if dist == 0:
                cores[0, mine].arrived()
            else:
                for d in (1, -1):
                    cores[dist, mine, d].arrived()

        return wait_group

    wait_g = gather_over_arc("G", mixers, 384, lambda: None)

    def cols_ready():
        pltpu.make_async_copy(cols.at[a, pl.ds(0, 15)], cols.at[a, pl.ds(0, 15)], bulk_recv.at[1]).wait()

    wait_c = gather_over_arc("C", cols, 16, cols_ready)

    def mix(arc):
        for c in range(3):
            unit = cols[arc, :, c * 16 : (c + 1) * 16, :].astype(jnp.float32).reshape(16, 2, 8, 256)
            b = jnp.concatenate([unit[:, 0].reshape(128, 256), unit[:, 1].reshape(128, 256)], axis=1).astype(jnp.bfloat16)
            q = jnp.dot(
                mixers[arc, c * 128 : (c + 1) * 128, :], jnp.concatenate([b, b], axis=0), preferred_element_type=jnp.float32
            )
            q = jnp.swapaxes(q.reshape(2, 8, 8, 512), 0, 1).reshape(8, 16, 512)
            high = q.astype(jnp.bfloat16)
            q_high[:, arc * 3 + c] = high
            q_low[:, arc * 3 + c] = (q - high.astype(jnp.float32)).astype(jnp.bfloat16)

    def mix_group(dist, mine):
        wait_g(dist, mine)
        wait_c(dist, mine)
        yl_of = yl if mine else 1 - yl
        if dist == 1:
            def body(k, _):
                dx = (k // 2) * 2 - 1
                mix(((x + dx + 4) % 4) * 4 + yl_of * 2 + k % 2)
                return 0
            lax.fori_loop(0, 4, body, 0)
        else:
            def body(k, _):
                mix(((x + dist) % 4) * 4 + yl_of * 2 + k)
                return 0
            lax.fori_loop(0, 2, body, 0)

    for dist in range(3):
        for mine in (True, False):
            at(("mix", dist, mine), lambda s=dist, m=mine: mix_group(s, m))

    def turn(dz):
        cross_late[dz].arrived()
        at_z = (z + dz + 8) % 8
        halves = []
        for h in range(2):
            sides = [
                rows[side * 8 + at_z].astype(jnp.float32).reshape(16, 3, 2, 8, 256)[:, :, h].reshape(48, 1, 8, 256)
                for side in range(2)
            ]
            halves.append(jnp.concatenate(sides, axis=1).reshape(768, 256))
        rows_t[at_z] = jnp.transpose(jnp.concatenate(halves, axis=1).astype(jnp.bfloat16))

    def clear():
        out_ref[...] = jnp.zeros_like(out_ref)

    at("clear", clear)
    for dz in cross_late:
        at(("turn", dz), lambda dz=dz: turn(dz))

    def accumulate(at_z):
        left = rows_t[at_z]
        right = jnp.concatenate([q_high[at_z].reshape(768, 512), q_low[at_z].reshape(768, 512)], axis=0)
        out_ref[...] += jnp.dot(jnp.concatenate([left, left], axis=1), right, preferred_element_type=jnp.float32)

    def accumulate_group(group):
        first, stride, count = group

        def body(k, _):
            accumulate((z + first + stride * k + 8) % 8)
            return 0

        lax.fori_loop(0, count, body, 0)

    for group in GROUPS:
        at(("sum", group), lambda g=group: accumulate_group(g))

    assert sorted(map(str, tasks)) == sorted(map(str, ORDER))
    for key in ORDER:
        tasks[key]()

    assert counter[0] <= N_SEM
    for n in (0, 1):
        pltpu.make_async_copy(blocks.at[pl.ds(0, 15)], blocks.at[pl.ds(0, 15)], bulk_send.at[n]).wait()
    for copy in started:
        copy.wait_send()


def on_device(partials, epoch_index, whitening):
    vmem = pl.BlockSpec(memory_space=pltpu.VMEM)
    return pl.pallas_call(
        kernel,
        out_shape=jax.ShapeDtypeStruct((512, 512), jnp.float32),
        in_specs=[pl.BlockSpec(memory_space=pl.ANY)] * 3,
        out_specs=vmem,
        scratch_shapes=[
            pltpu.VMEM((1, 3, 8, 8192), jnp.bfloat16),
            pltpu.VMEM((1, 128), jnp.int32),
            pltpu.VMEM((1, 3, 128, 128), jnp.float32),
            pltpu.SemaphoreType.DMA((3,)),
            pltpu.VMEM((16, 48, 256), jnp.bfloat16),
            pltpu.VMEM((16, 16, 48, 256), jnp.bfloat16),
            pltpu.VMEM((16, 16, 48, 256), jnp.bfloat16),
            pltpu.VMEM((16, 384, 256), jnp.bfloat16),
            pltpu.VMEM((8, 512, 768), jnp.bfloat16),
            pltpu.VMEM((8, 48, 16, 512), jnp.bfloat16),
            pltpu.VMEM((8, 48, 16, 512), jnp.bfloat16),
            pltpu.SemaphoreType.DMA((N_SEM,)),
            pltpu.SemaphoreType.DMA((N_SEM,)),
            pltpu.SemaphoreType.DMA((2,)),
            pltpu.SemaphoreType.DMA((2,)),
        ],
        compiler_params=pltpu.CompilerParams(
            collective_id=0, has_side_effects=True, vmem_limit_bytes=56 * 2**20
        ),
    )(partials, epoch_index, whitening)


def solution(mesh):
    placed = (P("arc", None, "par", None), P("arc", None), P("arc", None, None, None))
    return jax.shard_map(
        on_device, mesh=mesh, in_specs=placed, out_specs=P("arc", "par"), check_vma=False
    )
```

```python
import math

import jax
import jax.numpy as jnp
from jax import lax
from jax.experimental import pallas as pl
from jax.experimental.pallas import tpu as pltpu
from jax.sharding import PartitionSpec as P

KERNEL_GAIN = 8.0
MESH = pl.DeviceIdType.MESH
EARLY = 9
N_SEM = 80
GROUPS = ((-1, 1, 3), (-2, 4, 2), (-3, 6, 2), (4, 1, 1))
ORDER = (
    "clear", ("G", "begin"), ("G", 1, True, 1), ("G", 1, True, -1), "rows", ("C", "begin"), ("G", 2, True, 1),
    ("G", "yl"), "early", ("z", 1, "L", 1), ("late", 0), ("z", 1, "E0", -1), ("mix", 0, True), ("late", -1),
    ("G", 1, False, 1), ("z", 1, "L", -1), ("late", 1), ("G", 1, False, -1), ("C", 1, True, 1),
    ("z", 1, "E0", 1), ("C", 1, True, -1), ("mix", 1, True), ("G", 2, False, 1), ("G", 2, True, -1),
    ("C", "yl"), ("C", 2, True, -1), ("G", 2, False, -1), ("z", 1, "E1", -1), ("z", 1, "E1", 1),
    ("z", 2, "L", -1), ("late", 2), ("z", 2, "E0", 1), ("turn", 0), ("turn", -1), ("z", 2, "L", 1),
    ("late", -2), ("mix", 0, False), ("C", 2, True, 1), ("turn", 1), ("z", 2, "E0", -1), ("mix", 2, True),
    ("C", 1, False, -1), ("C", 1, False, 1), ("mix", 1, False), ("z", 3, "L", -1), ("late", 3),
    ("z", 3, "E0", 1), ("C", 2, False, 1), ("C", 2, False, -1), ("z", 2, "E1", -1), ("turn", 2),
    ("z", 3, "E0", -1), ("z", 3, "L", 1), ("late", -3), ("z", 2, "E1", 1), ("turn", -2), ("mix", 2, False),
    ("sum", (-1, 1, 3)), ("z", 4, "L", 1), ("z", 4, "L", -1), ("late", 4), ("z", 3, "E1", -1),
    ("z", 3, "E1", 1), ("sum", (-2, 4, 2)), ("turn", 3), ("turn", -3), ("z", 4, "E0", 1), ("z", 4, "E0", -1),
    ("sum", (-3, 6, 2)), ("z", 4, "E1", 1), ("z", 4, "E1", -1), ("turn", 4), ("sum", (4, 1, 1)),
)


def kernel(part_hbm, epoch_hbm, white_hbm, out_ref, part_ref, epoch_ref, white_ref, load_sem, blocks, rows, cols, mixers, rows_t, q_high, q_low, send_sem, recv_sem, bulk_send, bulk_recv):
    a = lax.axis_index("arc")
    p = lax.axis_index("par")
    x, yl, core = a // 4, (a // 2) % 2, a % 2
    yh, z = p // 8, p % 8
    other_core = (x * 4 + yl * 2 + 1 - core, p)
    yl_partner = (x * 4 + (1 - yl) * 2 + core, p)
    yh_partner = (a, (1 - yh) * 8 + z)

    def arc_at(dx, same_yl, same_core):
        return (
            ((x + dx + 4) % 4) * 4
            + (yl if same_yl else 1 - yl) * 2
            + (core if same_core else 1 - core)
        )

    def par_at(same_yh, dz):
        return (yh if same_yh else 1 - yh) * 8 + (z + dz + 8) % 8

    barrier = pltpu.get_barrier_semaphore()

    def greet(k, _):
        pl.semaphore_signal(barrier, inc=1, device_id=((a + k) % 16, p), device_id_type=MESH)
        pl.semaphore_signal(barrier, inc=1, device_id=(a, (p + k) % 16), device_id_type=MESH)
        return 0

    lax.fori_loop(1, 16, greet, 0)
    loads = [
        pltpu.make_async_copy(src, dst, load_sem.at[n])
        for n, (src, dst) in enumerate(((part_hbm, part_ref), (epoch_hbm, epoch_ref), (white_hbm, white_ref)))
    ]
    for load in loads:
        load.start()
    loads[0].wait()

    for c in range(3):
        for b in range(16):
            piece = part_ref[0, c, :, b * 512 : (b + 1) * 512].astype(jnp.float32)
            unit = jnp.concatenate([piece[:, :256], piece[:, 256:]], axis=0)
            blocks[b, c * 16 : (c + 1) * 16, :] = unit.astype(jnp.bfloat16)

    pl.semaphore_wait(barrier, 30)

    def send_rows(k, _):
        b = (a + k) % 16
        pltpu.make_async_remote_copy(
            src_ref=blocks.at[b], dst_ref=rows.at[p, a], send_sem=bulk_send.at[0], recv_sem=bulk_recv.at[0],
            device_id=(b, p), device_id_type=MESH,
        ).start()
        return 0

    def send_cols(k, _):
        b = (p + k) % 16
        pltpu.make_async_remote_copy(
            src_ref=blocks.at[b], dst_ref=cols.at[a, p], send_sem=bulk_send.at[1], recv_sem=bulk_recv.at[1],
            device_id=(a, b), device_id_type=MESH,
        ).start()
        return 0

    for k in range(1, 16):
        send_rows(k, 0)
    for k in range(1, 16):
        send_cols(k, 0)
    rows[p, a] = blocks[a]
    cols[a, p] = blocks[p]

    loads[1].wait()
    loads[2].wait()

    row_scale = 1.0 / math.sqrt(6144)
    times = epoch_ref[...].astype(jnp.float32) / jnp.float32(511)
    later = jnp.broadcast_to(times, (128, 128))
    earlier = jnp.transpose(later)
    i = lax.broadcasted_iota(jnp.int32, (128, 128), 0)
    j = lax.broadcasted_iota(jnp.int32, (128, 128), 1)
    eye = jnp.where(i == j, 1.0, 0.0).astype(jnp.float32)
    green = jnp.minimum(later, earlier) * (1.0 - jnp.maximum(later, earlier))
    integral = eye + KERNEL_GAIN / 128 * green
    for c in range(3):
        m = jnp.dot(white_ref[0, c], integral, precision=lax.Precision.HIGHEST, preferred_element_type=jnp.float32) * row_scale
        g = jnp.dot(jnp.transpose(m), m, precision=lax.Precision.HIGHEST, preferred_element_type=jnp.float32)
        high = g.astype(jnp.bfloat16)
        low = (g - high.astype(jnp.float32)).astype(jnp.bfloat16)
        mixers[a, c * 128 : (c + 1) * 128, :] = jnp.concatenate([high, low], axis=1)

    counter = [0]
    started = []

    class Link:
        def __init__(self, target, src, landing):
            self.n = counter[0]
            counter[0] += 1
            self.target, self.src, self.landing = target, src, landing

        def start(self):
            self.copy = pltpu.make_async_remote_copy(
                src_ref=self.src, dst_ref=self.src, send_sem=send_sem.at[self.n], recv_sem=recv_sem.at[self.n],
                device_id=self.target, device_id_type=MESH,
            )
            self.copy.start()
            started.append(self.copy)

        def arrived(self):
            pltpu.make_async_remote_copy(
                src_ref=self.landing, dst_ref=self.landing, send_sem=send_sem.at[self.n], recv_sem=recv_sem.at[self.n],
                device_id=self.target, device_id_type=MESH,
            ).wait_recv()

    tasks = {}

    def at(key, act):
        tasks[key] = act

    def row_part(part, dz, half=None):
        same = part != "E1"
        lo, n = (0, EARLY) if part in ("E0", "E1") else (EARLY, 16 - EARLY)
        if half is not None:
            n1 = n // 2
            lo, n = (lo, n1) if half == 0 else (lo + n1, n - n1)
        return rows.at[par_at(same, dz), pl.ds(lo, n)]

    parts = ("L", "E0", "E1")
    z_to = {1: (a, par_at(True, 1)), -1: (a, par_at(True, -1))}
    ring = {}
    for step in range(1, 5):
        for part in parts:
            for d in (1, -1):
                half = None if step < 4 else (0 if d == 1 else 1)
                ring[step, part, d] = Link(
                    z_to[d], row_part(part, -d * (step - 1), half), row_part(part, -d * step, half)
                )
    cross_early = Link(yh_partner, rows.at[p, pl.ds(0, EARLY)], rows.at[par_at(False, 0), pl.ds(0, EARLY)])
    late = pl.ds(EARLY, 16 - EARLY)
    cross_late = {
        dz: Link(yh_partner, rows.at[par_at(True, dz), late], rows.at[par_at(False, dz), late])
        for dz in (0, 1, -1, 2, -2, 3, -3, 4)
    }

    def rows_ready():
        pltpu.make_async_copy(rows.at[p, pl.ds(0, 15)], rows.at[p, pl.ds(0, 15)], bulk_recv.at[0]).wait()
        cross_early.start()
        for part in ("L", "E0"):
            for d in (1, -1):
                ring[1, part, d].start()

    at("rows", rows_ready)

    def early_crossed():
        cross_early.arrived()
        for d in (1, -1):
            ring[1, "E1", d].start()

    at("early", early_crossed)

    def ring_arrival(step, part, d):
        ring[step, part, d].arrived()
        if step < 4:
            ring[step + 1, part, d].start()

    for step in range(1, 5):
        for part in parts:
            for d in (1, -1):
                at(("z", step, part, d), lambda s=step, q=part, d=d: ring_arrival(s, q, d))

    for dz in cross_late:
        at(("late", dz), lambda dz=dz: cross_late[dz].start())

    def gather_over_arc(name, buf, extent, first):
        def piece(arc, half=None):
            if half is None:
                return buf.at[arc]
            n = extent // 2
            return buf.at[arc, pl.ds(half * n, n)]

        x_to = {1: (arc_at(1, True, True), p), -1: (arc_at(-1, True, True), p)}
        to_yl = Link(yl_partner, piece(a), piece(arc_at(0, False, True)))
        hops, cores = {}, {}
        for mine in (True, False):
            for d in (1, -1):
                hops[1, mine, d] = Link(x_to[d], piece(arc_at(0, mine, True)), piece(arc_at(-d, mine, True)))
                half = 0 if d == 1 else 1
                hops[2, mine, d] = Link(x_to[d], piece(arc_at(-d, mine, True), half), piece(arc_at(2, mine, True), half))
            cores[0, mine] = Link(other_core, piece(arc_at(0, mine, True)), piece(arc_at(0, mine, False)))
            for d in (1, -1):
                cores[1, mine, d] = Link(other_core, piece(arc_at(-d, mine, True)), piece(arc_at(-d, mine, False)))
                half = 0 if d == 1 else 1
                cores[2, mine, d] = Link(other_core, piece(arc_at(2, mine, True), half), piece(arc_at(2, mine, False), half))

        def begin():
            first()
            to_yl.start()
            for d in (1, -1):
                hops[1, True, d].start()
            cores[0, True].start()

        def yl_arrival():
            to_yl.arrived()
            for d in (1, -1):
                hops[1, False, d].start()
            cores[0, False].start()

        def hop_arrival(dist, mine, d):
            hops[dist, mine, d].arrived()
            if dist == 1:
                hops[2, mine, d].start()
            cores[dist, mine, d].start()

        at((name, "begin"), begin)
        at((name, "yl"), yl_arrival)
        for mine in (True, False):
            for dist in (1, 2):
                for d in (1, -1):
                    at((name, dist, mine, d), lambda s=dist, m=mine, d=d: hop_arrival(s, m, d))

        def wait_group(dist, mine):
            if dist == 0:
                cores[0, mine].arrived()
            else:
                for d in (1, -1):
                    cores[dist, mine, d].arrived()

        return wait_group

    wait_g = gather_over_arc("G", mixers, 384, lambda: None)

    def cols_ready():
        pltpu.make_async_copy(cols.at[a, pl.ds(0, 15)], cols.at[a, pl.ds(0, 15)], bulk_recv.at[1]).wait()

    wait_c = gather_over_arc("C", cols, 16, cols_ready)

    def mix(arc):
        for c in range(3):
            unit = cols[arc, :, c * 16 : (c + 1) * 16, :].astype(jnp.float32).reshape(16, 2, 8, 256)
            b = jnp.concatenate([unit[:, 0].reshape(128, 256), unit[:, 1].reshape(128, 256)], axis=1).astype(jnp.bfloat16)
            q = jnp.dot(
                mixers[arc, c * 128 : (c + 1) * 128, :], jnp.concatenate([b, b], axis=0), preferred_element_type=jnp.float32
            )
            q = jnp.swapaxes(q.reshape(2, 8, 8, 512), 0, 1).reshape(8, 16, 512)
            high = q.astype(jnp.bfloat16)
            q_high[:, arc * 3 + c] = high
            q_low[:, arc * 3 + c] = (q - high.astype(jnp.float32)).astype(jnp.bfloat16)

    def mix_group(dist, mine):
        wait_g(dist, mine)
        wait_c(dist, mine)
        yl_of = yl if mine else 1 - yl
        if dist == 1:
            def body(k, _):
                dx = (k // 2) * 2 - 1
                mix(((x + dx + 4) % 4) * 4 + yl_of * 2 + k % 2)
                return 0
            lax.fori_loop(0, 4, body, 0)
        else:
            def body(k, _):
                mix(((x + dist) % 4) * 4 + yl_of * 2 + k)
                return 0
            lax.fori_loop(0, 2, body, 0)

    for dist in range(3):
        for mine in (True, False):
            at(("mix", dist, mine), lambda s=dist, m=mine: mix_group(s, m))

    def turn(dz):
        cross_late[dz].arrived()
        at_z = (z + dz + 8) % 8
        halves = []
        for h in range(2):
            sides = [
                rows[side * 8 + at_z].astype(jnp.float32).reshape(16, 3, 2, 8, 256)[:, :, h].reshape(48, 1, 8, 256)
                for side in range(2)
            ]
            halves.append(jnp.concatenate(sides, axis=1).reshape(768, 256))
        rows_t[at_z] = jnp.transpose(jnp.concatenate(halves, axis=1).astype(jnp.bfloat16))

    def clear():
        out_ref[...] = jnp.zeros_like(out_ref)

    at("clear", clear)
    for dz in cross_late:
        at(("turn", dz), lambda dz=dz: turn(dz))

    def accumulate(at_z):
        left = rows_t[at_z]
        right = jnp.concatenate([q_high[at_z].reshape(768, 512), q_low[at_z].reshape(768, 512)], axis=0)
        out_ref[...] += jnp.dot(jnp.concatenate([left, left], axis=1), right, preferred_element_type=jnp.float32)

    def accumulate_group(group):
        first, stride, count = group

        def body(k, _):
            accumulate((z + first + stride * k + 8) % 8)
            return 0

        lax.fori_loop(0, count, body, 0)

    for group in GROUPS:
        at(("sum", group), lambda g=group: accumulate_group(g))

    assert sorted(map(str, tasks)) == sorted(map(str, ORDER))
    for key in ORDER:
        tasks[key]()

    assert counter[0] <= N_SEM
    for n in (0, 1):
        pltpu.make_async_copy(blocks.at[pl.ds(0, 15)], blocks.at[pl.ds(0, 15)], bulk_send.at[n]).wait()
    for copy in started:
        copy.wait_send()


def on_device(partials, epoch_index, whitening):
    vmem = pl.BlockSpec(memory_space=pltpu.VMEM)
    return pl.pallas_call(
        kernel,
        out_shape=jax.ShapeDtypeStruct((512, 512), jnp.float32),
        in_specs=[pl.BlockSpec(memory_space=pl.ANY)] * 3,
        out_specs=vmem,
        scratch_shapes=[
            pltpu.VMEM((1, 3, 8, 8192), jnp.bfloat16),
            pltpu.VMEM((1, 128), jnp.int32),
            pltpu.VMEM((1, 3, 128, 128), jnp.float32),
            pltpu.SemaphoreType.DMA((3,)),
            pltpu.VMEM((16, 48, 256), jnp.bfloat16),
            pltpu.VMEM((16, 16, 48, 256), jnp.bfloat16),
            pltpu.VMEM((16, 16, 48, 256), jnp.bfloat16),
            pltpu.VMEM((16, 384, 256), jnp.bfloat16),
            pltpu.VMEM((8, 512, 768), jnp.bfloat16),
            pltpu.VMEM((8, 48, 16, 512), jnp.bfloat16),
            pltpu.VMEM((8, 48, 16, 512), jnp.bfloat16),
            pltpu.SemaphoreType.DMA((N_SEM,)),
            pltpu.SemaphoreType.DMA((N_SEM,)),
            pltpu.SemaphoreType.DMA((2,)),
            pltpu.SemaphoreType.DMA((2,)),
        ],
        compiler_params=pltpu.CompilerParams(
            collective_id=0, has_side_effects=True, vmem_limit_bytes=56 * 2**20
        ),
    )(partials, epoch_index, whitening)


def solution(mesh):
    placed = (P("arc", None, "par", None), P("arc", None), P("arc", None, None, None))
    return jax.shard_map(
        on_device, mesh=mesh, in_specs=placed, out_specs=P("arc", "par"), check_vma=False
    )
```
